512 devices in a mesh: section: 16 (over z, x_hi), tensor: 32 (over x_lo, y, core).
Axes of the slice: x: 4 (x_hi: 2, x_lo: 2; x = x_hi * 2 + x_lo), y: 8, z: 8, core: 2. Of those that a mesh axis runs over, the one named last changes fastest.
Arguments:
- hidden: bfloat16 [4, 52, 4608], P(None, None, 'tensor'), may hold values from -6 to 6
- weight: bfloat16 [139264, 4608], P(('section', 'tensor')), may hold values from -1 to 1
- targets: int32 [4, 52], replicated, may hold values from 0 to 139263
- plan: int32 [4], replicated, may hold values from 0 to 3, each once
- row_grad: float32 [4, 52], replicated, may hold values from -4 to 4
Outputs:
- logprob: float32 [4, 52], replicated
- hidden_grad: bfloat16 [4, 52, 4608], P(None, None, 'tensor')
- weight_grad: bfloat16 [139264, 4608], P(('section', 'tensor'))
- target_scale: float32 [4, 52], replicated
The draws below stay inside these ranges and needn't reach their ends.
All inputs are finite; a program needn't handle non-finite values.
Results may differ from the reference program's by a relative error of at most 0.015.
Values may be sent and summed in bfloat16 or wider, within the bound.
A program may use at most 64 MiB of HBM per device.

```python
import math
import jax
import jax.numpy as jnp
import numpy as np
from jax import lax

D = 4608
V_DEV = 272
MICRO = 4
MROWS = 52
VOCAB = 139264
N_SECTION = 16
N_TENSOR = 32


def draw_weight(key, part):
    key = jax.random.fold_in(key, 11)
    normal_key, spread_key = jax.random.split(key, 2)
    values = jax.random.truncated_normal(normal_key, -4.0, 4.0, (VOCAB, D), jnp.float32)
    position = jnp.arange(VOCAB, dtype=jnp.float32) / VOCAB
    ramp = 0.55 + position
    spread = jnp.exp(jax.random.uniform(spread_key, (VOCAB,), jnp.float32, -0.2, 0.2))
    scaled = values * (ramp * spread)[:, None] * D ** (-0.5)
    return jnp.clip(scaled, -1.0, 1.0).astype(jnp.bfloat16)


def touch_ends(result, rng, least, top_value):
    dims = result.shape
    spot = [jax.random.randint(jax.random.fold_in(rng, axis), (), 0, dims[axis]) for axis in range(len(dims))]
    result = result.at[tuple(spot)].set(least)
    longest = dims.index(max(dims))
    spot[longest] = (spot[longest] + 1) % dims[longest]
    return result.at[tuple(spot)].set(top_value)


def block_levels(key, dims, cuts, smallest, largest):
    def one(dim, blocks):
        draws = jax.random.uniform(jax.random.fold_in(jax.random.fold_in(key, 6), dim), (blocks,), jnp.float32, smallest / len(cuts), largest / len(cuts))
        return jnp.repeat(jnp.exp(draws), dims[dim] // blocks).reshape((-1,) + (1,) * (len(dims) - dim - 1))

    level = one(*cuts[0])
    for cut in cuts[1:]:
        level = level * one(*cut)
    return level


def ranked_wide(rng, extent, amount, skew):
    weights = [min(1 << octave, amount + 1 - (1 << octave)) * (1 << 20) // math.isqrt((1 << octave) ** skew) + 1 for octave in range((amount + 1).bit_length()) if 1 << octave <= amount]
    scale = 1 + sum(weights) // (1 << 30)
    grid = np.cumsum(np.array([max(1, weight // scale) for weight in weights]))
    ticket = jax.random.randint(jax.random.fold_in(rng, 1), extent, 0, int(grid[len(weights) - 1]))
    start = jnp.left_shift(1, jnp.searchsorted(jnp.asarray(grid, jnp.int32), ticket, side="right").astype(jnp.int32))
    grade = start - 1 + jax.random.randint(jax.random.fold_in(rng, 4), extent, 0, 1 << 30) % jnp.minimum(start, amount + 1 - start)
    return jax.random.permutation(jax.random.fold_in(rng, 2), amount)[grade].astype(jnp.int32)


def normal_values(stream_key, dims, scale, reach, pieces=(), kind=jnp.bfloat16):
    array = scale * jax.random.normal(stream_key, dims, jnp.float32)
    if pieces:
        array = array * block_levels(stream_key, dims, pieces, -0.22, 0.18)
    return jnp.clip(array, -reach, reach).astype(kind)


def setup_inputs(seed: int = 0) -> dict:
    seeds = jax.random.split(jax.random.key(seed), 6)
    return {
        "hidden": normal_values(seeds[0], (MICRO, MROWS, D), 1.0, 6.0, ((2, 32),)),
        "weight": draw_weight(jax.random.fold_in(seeds[5], 71), 0),
        "targets": touch_ends(ranked_wide(seeds[2], (MICRO, MROWS), VOCAB, 2), jax.random.fold_in(seeds[2], 3), 0, VOCAB - 1).astype(jnp.int32),
        "plan": jax.random.permutation(seeds[3], MICRO).astype(jnp.int32),
        "row_grad": normal_values(seeds[4], (MICRO, MROWS), 1.0, 4.0, (), jnp.float32),
    }


softcap_value = 30.0


def reference(hidden, weight, targets, plan, row_grad):
    flat_rows = hidden.reshape(MICRO * MROWS, D)
    select = plan[:, None] == jnp.arange(MICRO, dtype=jnp.int32)[None, :]
    order_targets = jnp.sum(jnp.where(select[:, :, None], targets[None], 0), axis=1).reshape(-1)
    order_grad = jnp.sum(jnp.where(select[:, :, None], row_grad[None], jnp.float32(0.0)), axis=1).reshape(-1)
    block_rows = V_DEV * N_TENSOR
    blocks = weight.reshape(N_SECTION, block_rows, D)
    offsets = jnp.arange(N_SECTION, dtype=jnp.int32) * block_rows

    def forward(inputs):
        weight_block, offset = inputs
        raw_logits = lax.dot_general(flat_rows, weight_block, (((1,), (1,)), ((), ())), preferred_element_type=jnp.float32)
        capped = softcap_value * jnp.tanh(raw_logits / softcap_value)
        vocab_ids = offset + jnp.arange(block_rows, dtype=jnp.int32)
        target_hit = vocab_ids[None, :] == order_targets[:, None]
        return capped, jnp.sum(jnp.exp(capped), axis=1), jnp.sum(jnp.where(target_hit, capped, jnp.float32(0.0)), axis=1)

    capped_all, totals, target_parts = lax.map(forward, (blocks, offsets))
    total = jnp.sum(totals, axis=0)
    target_logit = jnp.sum(target_parts, axis=0)
    slot_logprob = (target_logit - jnp.log(total)).reshape(MICRO, MROWS)
    logprob = jnp.sum(jnp.where(select[:, :, None], slot_logprob[:, None, :], jnp.float32(0.0)), axis=0)
    slot_scale = (order_grad * (1.0 - jnp.square(target_logit / softcap_value))).reshape(MICRO, MROWS)
    target_scale = jnp.sum(jnp.where(select[:, :, None], slot_scale[:, None, :], jnp.float32(0.0)), axis=0)

    def backward(running, inputs):
        weight_block, offset, capped = inputs
        vocab_ids = offset + jnp.arange(block_rows, dtype=jnp.int32)
        target_hit = (vocab_ids[None, :] == order_targets[:, None]).astype(jnp.float32)
        probability = jnp.exp(capped) / total[:, None]
        curve = 1.0 - jnp.square(capped / softcap_value)
        scaled = order_grad[:, None] * (target_hit - probability)
        logit_grad = (scaled * curve).astype(jnp.bfloat16)
        negative = -(order_grad[:, None] * probability)
        soft_grad = (negative * curve).astype(jnp.bfloat16)
        running = running + jnp.dot(logit_grad, weight_block, preferred_element_type=jnp.float32)
        block_grad = lax.dot_general(soft_grad, flat_rows, (((0,), (0,)), ((), ())), preferred_element_type=jnp.float32)
        return running, block_grad.astype(jnp.bfloat16)

    summed, block_grads = lax.scan(backward, jnp.zeros((MICRO * MROWS, D), jnp.float32), (blocks, offsets, capped_all))
    hidden_grad = summed.reshape(MICRO, MROWS, D).astype(jnp.bfloat16)
    return logprob, hidden_grad, block_grads.reshape(VOCAB, D), target_scale
```

```python
import functools

import jax
import jax.numpy as jnp
from jax import lax
from jax.experimental import pallas as pl
from jax.experimental.pallas import tpu as pltpu
from jax.sharding import PartitionSpec as P

MESH = pl.DeviceIdType.MESH
CAP = 30.0
F32 = jnp.float32
BF16 = jnp.bfloat16
MICRO = 4
ROWS = 52
SLOT = 64
V = 272
D = 4608
SH = 144
NEAR = (1, 7, 2, 6, 3, 5, 4)
FAR = (4, 3, 5, 2, 6, 1, 7)


def coords():
    s = lax.axis_index("section")
    t = lax.axis_index("tensor")
    x_hi, z = lax.rem(s, 2), lax.div(s, 2)
    q, y, c = lax.div(t, 16), lax.rem(lax.div(t, 2), 8), lax.rem(t, 2)
    return x_hi * 2 + q, y, z, c


def dev(x, y, z, c):
    x, y, z, c = lax.rem(x + 4, 4), lax.rem(y + 8, 8), lax.rem(z + 8, 8), lax.rem(c + 2, 2)
    return (z * 2 + lax.div(x, 2), lax.rem(x, 2) * 16 + y * 2 + c)


def rcopy(src, dst, ss, rs, to):
    return pltpu.make_async_remote_copy(
        src_ref=src, dst_ref=dst, send_sem=ss, recv_sem=rs, device_id=to, device_id_type=MESH
    )


def slot_lanes(ref, plan_ref, fill, dtype):
    parts = []
    for k in range(MICRO):
        row = jnp.zeros((1, SLOT), dtype)
        for j in range(MICRO):
            row = jnp.where(plan_ref[k] == j, ref[pl.ds(j, 1), :], row)
        parts.append(row)
    wide = jnp.concatenate(parts, axis=1)
    lane = lax.broadcasted_iota(jnp.int32, (1, 4 * SLOT), 1)
    return jnp.where(lax.rem(lane, SLOT) < ROWS, wide, jnp.full_like(wide, fill))


def comm_kernel(
    hidden_ref, weight_ref, targets_ref, plan_ref, grad_ref,
    ht_ref, soft_ref, hg_ref, stat_ref,
    pad, h, w, wt, own, ctx, crx, xtx, xrx, ztx, zrx, ytx, yrx, rtx, rrx, atx, arx, tot_tx, tot_rx,
    w_sem, o_sem,
    gy_s, gy_r, gz_s, gz_r, gx_s, gx_r, gc_s, gc_r,
    t_s, t_r, c_s, c_r, x_s, x_r, z_s, z_r, y_s, y_r, r_s, r_r, a_s, a_r, b_s, b_r,
):
    x, y, z, c = coords()
    q, x_hi, p, zq = lax.rem(x, 2), lax.div(x, 2), lax.rem(z, 2), lax.div(z, 2)
    other = 1 - q
    me = q * 16 + y * 2 + c
    partner = dev(x, y, z, 1 - c)

    barrier = pltpu.get_barrier_semaphore()
    peers = [dev(x, y + d, z, c) for d in range(1, 8)]
    peers += [dev(x + a, y, z, c + b) for a in range(4) for b in range(2) if a or b]
    peers += [dev(x + 2 * a, y, z + d, c) for d in range(1, 8) for a in range(2)]
    for peer in peers:
        pl.semaphore_signal(barrier, inc=1, device_id=peer, device_id_type=MESH)
    w_copy = pltpu.make_async_copy(weight_ref, w, w_sem)
    w_copy.start()

    pad[...] = jnp.zeros_like(pad)
    for k in range(MICRO):
        pad[k * SLOT : k * SLOT + ROWS, 0:SH] = hidden_ref[k].astype(F32)
    mine = jnp.transpose(pad[...], (1, 0))[0:SH]
    h[0, me] = mine[:, 0:128].astype(BF16)
    h[1, me] = mine[:, 128:256].astype(BF16)
    slot_target = slot_lanes(targets_ref, plan_ref, -1, jnp.int32)
    slot_grad = slot_lanes(grad_ref, plan_ref, 0.0, F32)
    pl.semaphore_wait(barrier, len(peers))

    def shard(x_lo, yy):
        return x_lo * 16 + yy * 2 + c

    def y_copy(yy, to_y):
        t = shard(q, yy)
        return rcopy(h.at[p, t], h.at[p, t], gy_s.at[to_y], gy_r.at[yy], dev(x, to_y, z, c))

    def z_copy(yy, half):
        t = shard(q, yy)
        return rcopy(h.at[half, t], h.at[half, t], gz_s.at[yy], gz_r.at[yy], dev(x, y, z + 1 - 2 * lax.rem(yy, 2), c))

    def x_copy(x_lo, yy, half):
        t = shard(x_lo, yy)
        return rcopy(h.at[half, t], h.at[half, t], gx_s.at[half, yy], gx_r.at[half, yy], dev(x + 1 - 2 * half, y, z, c))

    def c_copy(x_lo, yy, cc, half):
        t = x_lo * 16 + yy * 2 + cc
        i = x_lo * 8 + yy
        return rcopy(h.at[half, t], h.at[half, t], gc_s.at[half, i], gc_r.at[half, i], partner)

    def at_y(d):
        return lax.rem(y + d, 8)

    for d in FAR:
        y_copy(y, at_y(d)).start()
    for half in range(2):
        x_copy(q, y, half).start()
        c_copy(q, y, c, half).start()
    w_copy.wait()
    for j in range(D // 128):
        wt[j * 128 : (j + 1) * 128, :] = jnp.transpose(w[:, j * 128 : (j + 1) * 128], (1, 0))
    for d in NEAR:
        yy = at_y(d)
        y_copy(yy, y).wait_recv()
        z_copy(yy, p).start()
        x_copy(q, yy, p).start()
        c_copy(q, yy, c, p).start()
    for d in NEAR:
        yy = at_y(d)
        z_copy(yy, 1 - p).wait_recv()
        x_copy(q, yy, 1 - p).start()
        c_copy(q, yy, c, 1 - p).start()
    for d in (0,) + NEAR:
        yy = at_y(d)
        for half in range(2):
            x_copy(other, yy, half).wait_recv()
            c_copy(other, yy, c, half).start()

    def block(b, raw):
        x_lo = lax.div(b, 2)
        for k in range(4):
            for half in range(2):
                c_copy(x_lo, lax.rem(b, 2) * 4 + k, 1 - c, half).wait_recv()
        cols = jnp.concatenate(
            [h[half, pl.ds(b * 8, 8)].reshape(8 * SH, 128) for half in range(2)], axis=1
        )
        part = w[:, pl.ds(pl.multiple_of(b * 8 * SH, 128), 8 * SH)]
        return raw + jnp.dot(part, cols, preferred_element_type=F32)

    def blocks(i, raw):
        return block(lax.rem(q * 2 + i, 4), raw)

    raw = lax.fori_loop(0, 4, blocks, jnp.zeros((V, 256), F32))
    ht_copy = pltpu.make_async_copy(h, ht_ref, o_sem)
    ht_copy.start()

    capped = CAP * jnp.tanh(raw / CAP)
    exponent = jnp.exp(capped)
    s_id, t_id = lax.axis_index("section"), lax.axis_index("tensor")
    ids = (s_id * 32 + t_id) * V + lax.broadcasted_iota(jnp.int32, (V, 256), 0)
    hit = ids == slot_target
    sums = jnp.concatenate(
        [
            jnp.sum(exponent, axis=0, keepdims=True),
            jnp.sum(jnp.where(hit, capped, 0.0), axis=0, keepdims=True),
        ],
        axis=0,
    )

    def exchange(stage, index, where, values):
        tot_tx[stage] = values
        tot_rx[stage, index] = values
        for d in FAR:
            rcopy(tot_tx.at[stage], tot_rx.at[stage, index], t_s.at[stage, d], t_r.at[stage, index], where(lax.rem(index + d, 8))).start()
        for d in FAR:
            j = lax.rem(index + d, 8)
            rcopy(tot_tx.at[stage], tot_rx.at[stage, j], t_s.at[stage, d], t_r.at[stage, j], where(j)).wait()
        total = tot_rx[stage, 0]
        for j in range(1, 8):
            total = total + tot_rx[stage, j]
        return total

    sums = exchange(0, x * 2 + c, lambda j: dev(lax.div(j, 2), y, z, lax.rem(j, 2)), sums)
    sums = exchange(1, y, lambda j: dev(x, j, z, c), sums)
    sums = exchange(2, z, lambda j: dev(x, y, j, c), sums)
    total, target_logit = sums[0:1], sums[1:2]

    bend = slot_grad * (1.0 - jnp.square(capped / CAP))
    prob = exponent / total
    logit_grad = (bend * (hit.astype(F32) - prob)).astype(BF16)

    def partial(t):
        rows = wt[pl.ds(pl.multiple_of(t * SH, 16), SH), :]
        return jnp.dot(rows, logit_grad, preferred_element_type=F32)

    def to_core(i):
        return rcopy(ctx.at[i], crx.at[i], c_s.at[i], c_r.at[i], partner)

    def send_core(i, _):
        i = lax.rem(other * 8 + i, 16)
        ctx[i] = partial(i * 2 + 1 - c).astype(BF16)
        to_core(i).start()
        return 0

    lax.fori_loop(0, 16, send_core, 0)

    def own_part(i, _):
        own[i] = partial(i * 2 + c)
        return 0

    lax.fori_loop(0, 16, own_part, 0)

    def to_x(yy, half):
        return rcopy(xtx.at[half, yy], xrx.at[half, yy], x_s.at[half, yy], x_r.at[half, yy], dev(x + 1 - 2 * half, y, z, c))

    def to_z(yy):
        return rcopy(ztx.at[yy], zrx.at[yy], z_s.at[yy], z_r.at[yy], dev(x, y, z + 1 - 2 * lax.rem(yy, 2), c))

    def to_y(frm, to):
        return rcopy(ytx.at[to], yrx.at[frm], y_s.at[to], y_r.at[frm], dev(x, to, z, c))

    def send_x(yy, _):
        i = other * 8 + yy
        to_core(i).wait_recv()
        both = own[i] + crx[i].astype(F32)
        for half in range(2):
            xtx[half, yy] = both[:, half * 128 : (half + 1) * 128].astype(BF16)
            to_x(yy, half).start()
        return 0

    lax.fori_loop(0, 8, send_x, 0)

    first = p == 0

    def send_z(k, _):
        yy = lax.rem(y + k, 8)
        i = q * 8 + yy
        to_core(i).wait_recv()
        to_x(yy, 0).wait_recv()
        to_x(yy, 1).wait_recv()
        both = own[i] + crx[i].astype(F32)
        low = both[:, 0:128] + xrx[0, yy].astype(F32)
        high = both[:, 128:256] + xrx[1, yy].astype(F32)
        ztx[yy] = jnp.where(first, high, low).astype(BF16)
        to_z(yy).start()
        own[i, :, 0:128] = jnp.where(first, low, high)
        return 0

    lax.fori_loop(0, 8, send_z, 0)

    def send_y(k, _):
        yy = lax.rem(y + k, 8)
        to_z(yy).wait_recv()
        ytx[yy] = (own[q * 8 + yy, :, 0:128] + zrx[yy].astype(F32)).astype(BF16)
        to_y(y, yy).start()
        return 0

    lax.fori_loop(1, 8, send_y, 0)
    to_z(y).wait_recv()
    acc = own[q * 8 + y, :, 0:128] + zrx[y].astype(F32)
    soft_ref[...] = (-(slot_grad * prob) * (1.0 - jnp.square(capped / CAP))).astype(BF16)
    for d in NEAR:
        yy = at_y(d)
        to_y(yy, y).wait_recv()
        acc = acc + yrx[yy].astype(F32)

    def member(j):
        return dev(2 * lax.rem(j, 2) + q, y, 2 * lax.div(j, 2) + p, c)

    index = zq * 2 + x_hi
    for j in range(8):
        rtx[j, 0:16] = acc[16 * j : 16 * j + 16].astype(BF16)
        rtx[j, 16:32] = acc[128:144].astype(BF16)

    def to_member(frm, to):
        return rcopy(rtx.at[to], rrx.at[frm], r_s.at[to], r_r.at[frm], member(to))

    for d in FAR:
        to_member(index, lax.rem(index + d, 8)).start()
    rrx[index] = rtx[index]
    for d in FAR:
        to_member(lax.rem(index + d, 8), index).wait_recv()
    done = rrx[0].astype(F32)
    for j in range(1, 8):
        done = done + rrx[j].astype(F32)
    atx[...] = done.astype(BF16)

    z2 = z + 1 - 2 * p
    slot = pl.ds(pl.multiple_of(index * 16, 16), 16)
    tail = pl.ds(128, 16)
    arx[p, slot] = atx[0:16]
    arx[p, tail] = atx[16:32]
    tail_copy = rcopy(atx.at[pl.ds(16, 16)], arx.at[p, tail], b_s, b_r, dev(x, y, z2, c))
    tail_copy.start()
    mates = [(a, d) for d in FAR + (0,) for a in range(2) if a or d]

    def to_mate(n, a, d):
        return rcopy(atx.at[pl.ds(0, 16)], arx.at[p, slot], a_s.at[n], a_r.at[n], dev(x + 2 * a, y, z + d, c))

    def from_mate(n, a, d):
        zz = lax.rem(z - d + 8, 8)
        pp = lax.rem(zz, 2)
        ii = lax.div(zz, 2) * 2 + lax.rem(x_hi + a, 2)
        there = pl.ds(pl.multiple_of(ii * 16, 16), 16)
        return rcopy(atx.at[pl.ds(0, 16)], arx.at[pp, there], a_s.at[n], a_r.at[n], dev(x + 2 * a, y, z - d, c))

    for n, (a, d) in enumerate(mates):
        to_mate(n, a, d).start()

    logprob = target_logit - jnp.log(total)
    scale = slot_grad * (1.0 - jnp.square(target_logit / CAP))
    stat_ref[...] = jnp.concatenate([logprob, scale], axis=0)

    for d in FAR:
        y_copy(y, at_y(d)).wait_send()
    for d in NEAR:
        z_copy(at_y(d), p).wait_send()
    for d in (0,) + NEAR:
        for half in range(2):
            x_copy(q, at_y(d), half).wait_send()
            for x_lo in range(2):
                c_copy(x_lo, at_y(d), c, half).wait_send()

    def drain(yy, _):
        to_core(yy).wait_send()
        to_core(yy + 8).wait_send()
        to_x(yy, 0).wait_send()
        to_x(yy, 1).wait_send()
        to_z(yy).wait_send()
        return 0

    lax.fori_loop(0, 8, drain, 0)
    for d in FAR:
        to_y(y, at_y(d)).wait_send()
        to_member(index, lax.rem(index + d, 8)).wait_send()
    ht_copy.wait()
    for n, (a, d) in enumerate(mates):
        from_mate(n, a, d).wait_recv()
        to_mate(n, a, d).wait_send()
    rcopy(atx.at[pl.ds(16, 16)], arx.at[1 - p, tail], b_s, b_r, dev(x, y, z2, c)).wait()
    hg_ref[...] = arx[...]


def finish_kernel(ht_ref, soft_ref, hg_ref, stat_ref, plan_ref, weight_grad_ref, hidden_grad_ref, logprob_ref, scale_ref):
    cols = jnp.concatenate([ht_ref[0], ht_ref[1]], axis=1)
    weight_grad_ref[...] = lax.dot_general(
        soft_ref[...], cols, (((1,), (1,)), ((), ())), preferred_element_type=F32
    ).astype(BF16)

    @pl.when(pl.program_id(0) == 0)
    def _():
        for half in range(2):
            grad = hg_ref[half].astype(F32)
            flat = jnp.transpose(jnp.concatenate([grad, jnp.zeros((112, 128), F32)], axis=0), (1, 0))
            for k in range(2):
                hidden_grad_ref[half * 2 + k] = flat[k * SLOT : k * SLOT + ROWS, 0:SH].astype(BF16)
        for row, out in enumerate((logprob_ref, scale_ref)):
            for m in range(MICRO):
                value = jnp.zeros((1, ROWS), F32)
                for k in range(MICRO):
                    value = jnp.where(plan_ref[k] == m, stat_ref[row : row + 1, k * SLOT : k * SLOT + ROWS], value)
                out[m : m + 1, :] = value


def per_device(hidden, weight, targets, plan, row_grad):
    vmem = pl.BlockSpec(memory_space=pltpu.VMEM)
    smem = pl.BlockSpec(memory_space=pltpu.SMEM)
    hbm = pl.BlockSpec(memory_space=pl.ANY)
    dma = pltpu.SemaphoreType.DMA
    piece = (SH, 128)
    targets = jnp.pad(targets, ((0, 0), (0, SLOT - ROWS)))
    row_grad = jnp.pad(row_grad, ((0, 0), (0, SLOT - ROWS)))
    ht, soft, hg, stat = pl.pallas_call(
        comm_kernel,
        out_shape=(
            jax.ShapeDtypeStruct((2, 32) + piece, BF16),
            jax.ShapeDtypeStruct((V, 256), BF16),
            jax.ShapeDtypeStruct((2,) + piece, BF16),
            jax.ShapeDtypeStruct((2, 256), F32),
        ),
        in_specs=[vmem, hbm, vmem, smem, vmem],
        out_specs=(hbm, vmem, vmem, vmem),
        scratch_shapes=[
            pltpu.VMEM((256, 256), F32),
            pltpu.VMEM((2, 32) + piece, BF16),
            pltpu.VMEM((V, D), BF16),
            pltpu.VMEM((D, V), BF16),
            pltpu.VMEM((16, SH, 256), F32),
            pltpu.VMEM((16, SH, 256), BF16),
            pltpu.VMEM((16, SH, 256), BF16),
            pltpu.VMEM((2, 8) + piece, BF16),
            pltpu.VMEM((2, 8) + piece, BF16),
            pltpu.VMEM((8,) + piece, BF16),
            pltpu.VMEM((8,) + piece, BF16),
            pltpu.VMEM((8,) + piece, BF16),
            pltpu.VMEM((8,) + piece, BF16),
            pltpu.VMEM((8, 32, 128), BF16),
            pltpu.VMEM((8, 32, 128), BF16),
            pltpu.VMEM((32, 128), BF16),
            pltpu.VMEM((2,) + piece, BF16),
            pltpu.VMEM((3, 2, 256), F32),
            pltpu.VMEM((3, 8, 2, 256), F32),
            dma, dma,
            dma((8,)), dma((8,)), dma((8,)), dma((8,)), dma((2, 8)), dma((2, 8)), dma((2, 16)), dma((2, 16)),
            dma((3, 8)), dma((3, 8)), dma((16,)), dma((16,)), dma((2, 8)), dma((2, 8)), dma((8,)), dma((8,)),
            dma((8,)), dma((8,)), dma((8,)), dma((8,)), dma((15,)), dma((15,)), dma, dma,
        ],
        compiler_params=pltpu.CompilerParams(collective_id=0, has_side_effects=True, vmem_limit_bytes=44 << 20),
        name="gather_logits_reduce",
    )(hidden, weight, targets, plan, row_grad)
    chunk = 1152
    weight_grad, hidden_grad, logprob, scale = pl.pallas_call(
        finish_kernel,
        grid=(D // chunk,),
        out_shape=(
            jax.ShapeDtypeStruct((V, D), BF16),
            jax.ShapeDtypeStruct((MICRO, ROWS, SH), BF16),
            jax.ShapeDtypeStruct((MICRO, ROWS), F32),
            jax.ShapeDtypeStruct((MICRO, ROWS), F32),
        ),
        in_specs=[
            pl.BlockSpec((2, chunk, 128), lambda i: (0, i, 0)),
            pl.BlockSpec((V, 256), lambda i: (0, 0)),
            pl.BlockSpec((2,) + piece, lambda i: (0, 0, 0)),
            pl.BlockSpec((2, 256), lambda i: (0, 0)),
            smem,
        ],
        out_specs=(
            pl.BlockSpec((V, chunk), lambda i: (0, i)),
            pl.BlockSpec((MICRO, ROWS, SH), lambda i: (0, 0, 0)),
            pl.BlockSpec((MICRO, ROWS), lambda i: (0, 0)),
            pl.BlockSpec((MICRO, ROWS), lambda i: (0, 0)),
        ),
        compiler_params=pltpu.CompilerParams(vmem_limit_bytes=32 << 20),
        name="weight_gradient",
    )(ht.reshape(2, D, 128), soft, hg, stat, plan)
    return logprob, hidden_grad, weight_grad, scale


def solution(mesh):
    placed = (P(None, None, "tensor"), P(("section", "tensor"), None), P(), P(), P())
    return jax.shard_map(
        per_device,
        mesh=mesh,
        in_specs=placed,
        out_specs=(P(), P(None, None, "tensor"), P(("section", "tensor"), None), P()),
        check_vma=False,
    )
```

```python
import functools

import jax
import jax.numpy as jnp
from jax import lax
from jax.experimental import pallas as pl
from jax.experimental.pallas import tpu as pltpu
from jax.sharding import PartitionSpec as P

MESH = pl.DeviceIdType.MESH
CAP = 30.0
F32 = jnp.float32
BF16 = jnp.bfloat16
MICRO = 4
ROWS = 52
SLOT = 64
V = 272
D = 4608
SH = 144
NEAR = (1, 7, 2, 6, 3, 5, 4)
FAR = (4, 3, 5, 2, 6, 1, 7)


def coords():
    s = lax.axis_index("section")
    t = lax.axis_index("tensor")
    x_hi, z = lax.rem(s, 2), lax.div(s, 2)
    q, y, c = lax.div(t, 16), lax.rem(lax.div(t, 2), 8), lax.rem(t, 2)
    return x_hi * 2 + q, y, z, c


def dev(x, y, z, c):
    x, y, z, c = lax.rem(x + 4, 4), lax.rem(y + 8, 8), lax.rem(z + 8, 8), lax.rem(c + 2, 2)
    return (z * 2 + lax.div(x, 2), lax.rem(x, 2) * 16 + y * 2 + c)


def rcopy(src, dst, ss, rs, to):
    return pltpu.make_async_remote_copy(
        src_ref=src, dst_ref=dst, send_sem=ss, recv_sem=rs, device_id=to, device_id_type=MESH
    )


def slot_lanes(ref, wide, plan_ref, fill, dtype):
    wide[...] = jnp.zeros_like(wide)
    wide[:, 0:ROWS] = ref[...]
    parts = []
    for k in range(MICRO):
        row = jnp.zeros((1, SLOT), dtype)
        for j in range(MICRO):
            row = jnp.where(plan_ref[k] == j, wide[j : j + 1, 0:SLOT], row)
        parts.append(row)
    flat = jnp.concatenate(parts, axis=1)
    lane = lax.broadcasted_iota(jnp.int32, (1, 4 * SLOT), 1)
    return jnp.where(lax.rem(lane, SLOT) < ROWS, flat, jnp.full_like(flat, fill))


def comm_kernel(
    hidden_ref, weight_ref, targets_ref, plan_ref, grad_ref,
    weight_grad_ref, hidden_grad_ref, logprob_ref, scale_ref,
    hid, tgt, grd, pln, tgt_wide, grd_wide, spread, pad, h, w, wt, wg,
    own, ctx, crx, xtx, xrx, ztx, zrx, own_t, ctx_t, crx_t, xtx_t, xrx_t, ztx_t, zrx_t,
    ytx, yrx, rtx, rrx, atx, arx, tot_tx, tot_rx,
    in_sem, o_sem,
    gy_s, gy_r, gz_s, gz_r, gx_s, gx_r, gc_s, gc_r,
    t_s, t_r, c_s, c_r, x_s, x_r, z_s, z_r, ct_s, ct_r, xt_s, xt_r, zt_s, zt_r,
    y_s, y_r, r_s, r_r, a_s, a_r, b_s, b_r,
):
    x, y, z, c = coords()
    q, x_hi, p, zq = lax.rem(x, 2), lax.div(x, 2), lax.rem(z, 2), lax.div(z, 2)
    other = 1 - q
    first = p == 0
    me = q * 16 + y * 2 + c
    partner = dev(x, y, z, 1 - c)

    barrier = pltpu.get_barrier_semaphore()
    peers = [dev(x, y + d, z, c) for d in range(1, 8)]
    peers += [dev(x + a, y, z, c + b) for a in range(4) for b in range(2) if a or b]
    peers += [dev(x + 2 * a, y, z + d, c) for d in range(1, 8) for a in range(2)]
    loads = [
        pltpu.make_async_copy(src, dst, in_sem.at[i])
        for i, (src, dst) in enumerate(
            ((hidden_ref, hid), (plan_ref, pln), (targets_ref, tgt), (grad_ref, grd), (weight_ref, w))
        )
    ]
    for load in loads:
        load.start()
    for peer in peers:
        pl.semaphore_signal(barrier, inc=1, device_id=peer, device_id_type=MESH)

    for load in loads[:4]:
        load.wait()
    spread[...] = hid[...].astype(F32)
    pad[...] = jnp.zeros_like(pad)
    for k in range(MICRO):
        pad[k * SLOT : k * SLOT + ROWS, 0:SH] = spread[:, k, :]
    mine = jnp.transpose(pad[...], (1, 0))[0:SH]
    h[0, me] = mine[:, 0:128].astype(BF16)
    h[1, me] = mine[:, 128:256].astype(BF16)
    slot_target = slot_lanes(tgt, tgt_wide, pln, -1, jnp.int32)
    slot_grad = slot_lanes(grd, grd_wide, pln, 0.0, F32)
    s_id, t_id = lax.axis_index("section"), lax.axis_index("tensor")
    ids = (s_id * 32 + t_id) * V + lax.broadcasted_iota(jnp.int32, (V, 256), 0)
    hit = ids == slot_target
    hot = hit.astype(F32).astype(BF16)

    loads[4].wait()
    for j in range(D // 128):
        wt[j * 128 : (j + 1) * 128, :] = jnp.transpose(w[:, j * 128 : (j + 1) * 128], (1, 0))

    def partial(t, terms):
        rows = wt[pl.ds(pl.multiple_of(t * SH, 16), SH), :]
        return jnp.dot(rows, terms, preferred_element_type=F32)

    def target_part(i, _):
        ctx_t[i] = partial(i * 2 + 1 - c, hot).astype(BF16)
        own_t[i] = partial(i * 2 + c, hot).astype(BF16)
        return 0

    lax.fori_loop(0, 16, target_part, 0)
    pl.semaphore_wait(barrier, len(peers))

    def shard(x_lo, yy):
        return x_lo * 16 + yy * 2 + c

    def y_copy(yy, to_y):
        t = shard(q, yy)
        return rcopy(h.at[p, t], h.at[p, t], gy_s.at[to_y], gy_r.at[yy], dev(x, to_y, z, c))

    def z_copy(yy, half):
        t = shard(q, yy)
        return rcopy(h.at[half, t], h.at[half, t], gz_s.at[yy], gz_r.at[yy], dev(x, y, z + 1 - 2 * lax.rem(yy, 2), c))

    def x_copy(x_lo, yy, half):
        t = shard(x_lo, yy)
        return rcopy(h.at[half, t], h.at[half, t], gx_s.at[half, yy], gx_r.at[half, yy], dev(x + 1 - 2 * half, y, z, c))

    def c_copy(x_lo, yy, cc, half):
        t = x_lo * 16 + yy * 2 + cc
        i = x_lo * 8 + yy
        return rcopy(h.at[half, t], h.at[half, t], gc_s.at[half, i], gc_r.at[half, i], partner)

    def to_core(i):
        return rcopy(ctx.at[i], crx.at[i], c_s.at[i], c_r.at[i], partner)

    def to_core_t(i):
        return rcopy(ctx_t.at[i], crx_t.at[i], ct_s.at[i], ct_r.at[i], partner)

    def to_x(yy, half):
        return rcopy(xtx.at[half, yy], xrx.at[half, yy], x_s.at[half, yy], x_r.at[half, yy], dev(x + 1 - 2 * half, y, z, c))

    def to_x_t(yy, half):
        return rcopy(xtx_t.at[half, yy], xrx_t.at[half, yy], xt_s.at[half, yy], xt_r.at[half, yy], dev(x + 1 - 2 * half, y, z, c))

    def to_z(yy):
        return rcopy(ztx.at[yy], zrx.at[yy], z_s.at[yy], z_r.at[yy], dev(x, y, z + 1 - 2 * lax.rem(yy, 2), c))

    def to_z_t(yy):
        return rcopy(ztx_t.at[yy], zrx_t.at[yy], zt_s.at[yy], zt_r.at[yy], dev(x, y, z + 1 - 2 * lax.rem(yy, 2), c))

    def to_y(frm, to):
        return rcopy(ytx.at[to], yrx.at[frm], y_s.at[to], y_r.at[frm], dev(x, to, z, c))

    def at_y(d):
        return lax.rem(y + d, 8)

    def send_x_t(yy, _):
        i = other * 8 + yy
        to_core_t(i).wait_recv()
        both = own_t[i].astype(F32) + crx_t[i].astype(F32)
        for half in range(2):
            xtx_t[half, yy] = both[:, half * 128 : (half + 1) * 128].astype(BF16)
            to_x_t(yy, half).start()
        return 0

    for d in FAR:
        y_copy(y, at_y(d)).start()
    for half in range(2):
        x_copy(q, y, half).start()
        c_copy(q, y, c, half).start()

    def start_core_t(i, _):
        to_core_t(lax.rem(other * 8 + i, 16)).start()
        return 0

    lax.fori_loop(0, 16, start_core_t, 0)
    lax.fori_loop(0, 4, send_x_t, 0)
    for d in NEAR:
        yy = at_y(d)
        y_copy(yy, y).wait_recv()
        z_copy(yy, p).start()
        x_copy(q, yy, p).start()
        c_copy(q, yy, c, p).start()
    for d in NEAR:
        yy = at_y(d)
        z_copy(yy, 1 - p).wait_recv()
        x_copy(q, yy, 1 - p).start()
        c_copy(q, yy, c, 1 - p).start()
    for d in (0,) + NEAR:
        yy = at_y(d)
        for half in range(2):
            x_copy(other, yy, half).wait_recv()
            c_copy(other, yy, c, half).start()
    lax.fori_loop(4, 8, send_x_t, 0)

    def columns(b):
        return jnp.concatenate(
            [h[half, pl.ds(b * 8, 8)].reshape(8 * SH, 128) for half in range(2)], axis=1
        )

    def blocks(i, raw):
        b = lax.rem(q * 2 + i, 4)
        x_lo = lax.div(b, 2)
        for k in range(4):
            for half in range(2):
                c_copy(x_lo, lax.rem(b, 2) * 4 + k, 1 - c, half).wait_recv()
        part = w[:, pl.ds(pl.multiple_of(b * 8 * SH, 128), 8 * SH)]
        return raw + jnp.dot(part, columns(b), preferred_element_type=F32)

    raw = lax.fori_loop(0, 4, blocks, jnp.zeros((V, 256), F32))
    capped = CAP * jnp.tanh(raw / CAP)
    exponent = jnp.exp(capped)
    curve = 1.0 - jnp.square(capped / CAP)
    sums = jnp.concatenate(
        [
            jnp.sum(exponent, axis=0, keepdims=True),
            jnp.sum(jnp.where(hit, capped, 0.0), axis=0, keepdims=True),
        ],
        axis=0,
    )

    def member_of(stage, j):
        if stage == 0:
            return dev(lax.div(j, 2), y, z, lax.rem(j, 2))
        return dev(x, j, z, c) if stage == 1 else dev(x, y, j, c)

    index_of = (x * 2 + c, y, z)

    def tot_copy(stage, frm, d):
        to = member_of(stage, lax.rem(index_of[stage] + d, 8))
        return rcopy(tot_tx.at[stage], tot_rx.at[stage, frm], t_s.at[stage, d], t_r.at[stage, frm], to)

    def begin(stage, values):
        tot_tx[stage] = values
        tot_rx[stage, index_of[stage]] = values
        for d in FAR:
            tot_copy(stage, index_of[stage], d).start()

    def end(stage):
        for d in FAR:
            tot_copy(stage, lax.rem(index_of[stage] + d, 8), d).wait()
        total = tot_rx[stage, 0]
        for j in range(1, 8):
            total = total + tot_rx[stage, j]
        return total

    begin(0, sums)
    terms = jnp.where(hit, 0.0, exponent * curve).astype(BF16)

    def send_core(i, _):
        ctx[i] = partial(i * 2 + 1 - c, terms).astype(BF16)
        to_core(i).start()
        return 0

    def own_part(i, _):
        own[i] = partial(i * 2 + c, terms)
        return 0

    lax.fori_loop(other * 8, other * 8 + 8, send_core, 0)
    lax.fori_loop(other * 8, other * 8 + 8, own_part, 0)

    def send_x(yy, _):
        i = other * 8 + yy
        to_core(i).wait_recv()
        both = own[i] + crx[i].astype(F32)
        for half in range(2):
            xtx[half, yy] = both[:, half * 128 : (half + 1) * 128].astype(BF16)
            to_x(yy, half).start()
        return 0

    lax.fori_loop(0, 8, send_x, 0)
    begin(1, end(0))
    lax.fori_loop(q * 8, q * 8 + 8, send_core, 0)
    lax.fori_loop(q * 8, q * 8 + 8, own_part, 0)

    def send_z_t(k, _):
        yy = lax.rem(y + k, 8)
        i = q * 8 + yy
        to_core_t(i).wait_recv()
        to_x_t(yy, 0).wait_recv()
        to_x_t(yy, 1).wait_recv()
        both = own_t[i].astype(F32) + crx_t[i].astype(F32)
        low = both[:, 0:128] + xrx_t[0, yy].astype(F32)
        high = both[:, 128:256] + xrx_t[1, yy].astype(F32)
        ztx_t[yy] = jnp.where(first, high, low).astype(BF16)
        to_z_t(yy).start()
        own_t[i, :, 0:128] = jnp.where(first, low, high).astype(BF16)
        return 0

    lax.fori_loop(0, 8, send_z_t, 0)
    begin(2, end(1))

    def send_z(k, _):
        yy = lax.rem(y + k, 8)
        i = q * 8 + yy
        to_core(i).wait_recv()
        to_x(yy, 0).wait_recv()
        to_x(yy, 1).wait_recv()
        both = own[i] + crx[i].astype(F32)
        low = both[:, 0:128] + xrx[0, yy].astype(F32)
        high = both[:, 128:256] + xrx[1, yy].astype(F32)
        ztx[yy] = jnp.where(first, high, low).astype(BF16)
        to_z(yy).start()
        own[i, :, 0:128] = jnp.where(first, low, high)
        return 0

    lax.fori_loop(0, 8, send_z, 0)
    sums = end(2)
    total, target_logit = sums[0:1], sums[1:2]
    target_curve = 1.0 - jnp.square(target_logit / CAP)
    coef_t = slot_grad * (1.0 - jnp.exp(target_logit) / total) * target_curve
    coef_s = slot_grad / total
    half_t = jnp.where(first, coef_t[:, 0:128], coef_t[:, 128:256])
    half_s = jnp.where(first, coef_s[:, 0:128], coef_s[:, 128:256])

    def merged(yy):
        to_z(yy).wait_recv()
        to_z_t(yy).wait_recv()
        i = q * 8 + yy
        soft_sum = own[i, :, 0:128] + zrx[yy].astype(F32)
        target_sum = own_t[i, :, 0:128].astype(F32) + zrx_t[yy].astype(F32)
        return half_t * target_sum - half_s * soft_sum

    def send_y(k, _):
        yy = lax.rem(y + k, 8)
        ytx[yy] = merged(yy).astype(BF16)
        to_y(y, yy).start()
        return 0

    lax.fori_loop(1, 8, send_y, 0)
    acc = merged(y)

    soft = (-(slot_grad * (exponent / total)) * curve).astype(BF16)

    def grad_block(b, _):
        wg[:, pl.ds(pl.multiple_of(b * 8 * SH, 128), 8 * SH)] = lax.dot_general(
            soft, columns(b), (((1,), (1,)), ((), ())), preferred_element_type=F32
        ).astype(BF16)
        return 0

    lax.fori_loop(0, 4, grad_block, 0)
    wg_copy = pltpu.make_async_copy(wg, weight_grad_ref, o_sem)
    wg_copy.start()
    logprob = target_logit - jnp.log(total)
    scale = slot_grad * target_curve
    for m in range(MICRO):
        for value, out in ((logprob, logprob_ref), (scale, scale_ref)):
            row = jnp.zeros((1, ROWS), F32)
            for k in range(MICRO):
                row = jnp.where(pln[k] == m, value[:, k * SLOT : k * SLOT + ROWS], row)
            out[m : m + 1, :] = row

    for d in NEAR:
        yy = at_y(d)
        to_y(yy, y).wait_recv()
        acc = acc + yrx[yy].astype(F32)

    def member(j):
        return dev(2 * lax.rem(j, 2) + q, y, 2 * lax.div(j, 2) + p, c)

    index = zq * 2 + x_hi
    for j in range(8):
        rtx[j, 0:16] = acc[16 * j : 16 * j + 16].astype(BF16)
        rtx[j, 16:32] = acc[128:144].astype(BF16)

    def to_member(frm, to):
        return rcopy(rtx.at[to], rrx.at[frm], r_s.at[to], r_r.at[frm], member(to))

    for d in FAR:
        to_member(index, lax.rem(index + d, 8)).start()
    rrx[index] = rtx[index]
    for d in FAR:
        to_member(lax.rem(index + d, 8), index).wait_recv()
    done = rrx[0].astype(F32)
    for j in range(1, 8):
        done = done + rrx[j].astype(F32)
    atx[...] = done.astype(BF16)

    z2 = z + 1 - 2 * p
    slot = pl.ds(pl.multiple_of(index * 16, 16), 16)
    tail = pl.ds(128, 16)
    arx[p, slot] = atx[0:16]
    arx[p, tail] = atx[16:32]
    tail_copy = rcopy(atx.at[pl.ds(16, 16)], arx.at[p, tail], b_s, b_r, dev(x, y, z2, c))
    tail_copy.start()
    mates = [(a, d) for d in FAR + (0,) for a in range(2) if a or d]

    def to_mate(n, a, d):
        return rcopy(atx.at[pl.ds(0, 16)], arx.at[p, slot], a_s.at[n], a_r.at[n], dev(x + 2 * a, y, z + d, c))

    def from_mate(n, a, d):
        zz = lax.rem(z - d + 8, 8)
        pp = lax.rem(zz, 2)
        ii = lax.div(zz, 2) * 2 + lax.rem(x_hi + a, 2)
        there = pl.ds(pl.multiple_of(ii * 16, 16), 16)
        return rcopy(atx.at[pl.ds(0, 16)], arx.at[pp, there], a_s.at[n], a_r.at[n], dev(x + 2 * a, y, z - d, c))

    for n, (a, d) in enumerate(mates):
        to_mate(n, a, d).start()

    for d in FAR:
        y_copy(y, at_y(d)).wait_send()
    for d in NEAR:
        z_copy(at_y(d), p).wait_send()
    for d in (0,) + NEAR:
        for half in range(2):
            x_copy(q, at_y(d), half).wait_send()
            for x_lo in range(2):
                c_copy(x_lo, at_y(d), c, half).wait_send()

    def drain(yy, _):
        for base in range(2):
            to_core(yy + 8 * base).wait_send()
            to_core_t(yy + 8 * base).wait_send()
            to_x(yy, base).wait_send()
            to_x_t(yy, base).wait_send()
        to_z(yy).wait_send()
        to_z_t(yy).wait_send()
        return 0

    lax.fori_loop(0, 8, drain, 0)
    for d in FAR:
        to_y(y, at_y(d)).wait_send()
        to_member(index, lax.rem(index + d, 8)).wait_send()
    wg_copy.wait()
    for n, (a, d) in enumerate(mates):
        from_mate(n, a, d).wait_recv()
        to_mate(n, a, d).wait_send()
    rcopy(atx.at[pl.ds(16, 16)], arx.at[1 - p, tail], b_s, b_r, dev(x, y, z2, c)).wait()
    for half in range(2):
        wide = jnp.concatenate([arx[half].astype(F32), jnp.zeros((256 - SH, 128), F32)], axis=0)
        flat = jnp.transpose(wide, (1, 0))
        for k in range(2):
            spread[:, half * 2 + k, :] = flat[k * SLOT : k * SLOT + ROWS, 0:SH]
    hidden_grad_ref[...] = spread[...].astype(BF16)


def hand_on_kernel(a0, a1, a2, a3, b0, b1, b2, b3, v0, v1, v2, v3, sem_in, sem_out):
    cuts = [(0, 64), (64, 64), (128, 64), (192, 80)]
    pieces = [(a0.at[pl.ds(i, n)], v0.at[pl.ds(i, n)], b0.at[pl.ds(i, n)]) for i, n in cuts]
    pieces += [(a1, v1, b1), (a2, v2, b2), (a3, v3, b3)]
    reads = [pltpu.make_async_copy(a, v, sem_in.at[i]) for i, (a, v, b) in enumerate(pieces)]
    writes = [pltpu.make_async_copy(v, b, sem_out.at[i]) for i, (a, v, b) in enumerate(pieces)]
    for read in reads:
        read.start()
    for read, write in zip(reads, writes):
        read.wait()
        write.start()
    for write in writes:
        write.wait()


def per_device(hidden, weight, targets, plan, row_grad):
    vmem = pl.BlockSpec(memory_space=pltpu.VMEM)
    hbm = pl.BlockSpec(memory_space=pl.ANY)
    dma = pltpu.SemaphoreType.DMA
    piece = (SH, 128)
    outs = (
        jax.ShapeDtypeStruct((V, D), BF16),
        jax.ShapeDtypeStruct((ROWS, MICRO, SH), BF16),
        jax.ShapeDtypeStruct((MICRO, ROWS), F32),
        jax.ShapeDtypeStruct((MICRO, ROWS), F32),
    )
    def buf(*shape, dtype=BF16):
        return pltpu.VMEM(shape, dtype)

    results = pl.pallas_call(
        comm_kernel,
        out_shape=outs,
        in_specs=[hbm] * 5,
        out_specs=(hbm, vmem, vmem, vmem),
        scratch_shapes=[
            buf(ROWS, MICRO, SH), buf(MICRO, ROWS, dtype=jnp.int32), buf(MICRO, ROWS, dtype=F32),
            pltpu.SMEM((MICRO,), jnp.int32),
            buf(MICRO, 128, dtype=jnp.int32), buf(MICRO, 128, dtype=F32),
            buf(ROWS, MICRO, SH, dtype=F32), buf(256, 256, dtype=F32),
            buf(2, 32, *piece), buf(V, D), buf(D, V), buf(V, D),
            buf(16, SH, 256, dtype=F32), buf(16, SH, 256), buf(16, SH, 256),
            buf(2, 8, *piece), buf(2, 8, *piece), buf(8, *piece), buf(8, *piece),
            buf(16, SH, 256), buf(16, SH, 256), buf(16, SH, 256),
            buf(2, 8, *piece), buf(2, 8, *piece), buf(8, *piece), buf(8, *piece),
            buf(8, *piece), buf(8, *piece), buf(8, 32, 128), buf(8, 32, 128), buf(32, 128), buf(2, *piece),
            buf(3, 2, 256, dtype=F32), buf(3, 8, 2, 256, dtype=F32),
            dma((5,)), dma,
            dma((8,)), dma((8,)), dma((8,)), dma((8,)), dma((2, 8)), dma((2, 8)), dma((2, 16)), dma((2, 16)),
            dma((3, 8)), dma((3, 8)), dma((16,)), dma((16,)), dma((2, 8)), dma((2, 8)), dma((8,)), dma((8,)),
            dma((16,)), dma((16,)), dma((2, 8)), dma((2, 8)), dma((8,)), dma((8,)),
            dma((8,)), dma((8,)), dma((8,)), dma((8,)), dma((15,)), dma((15,)), dma, dma,
        ],
        compiler_params=pltpu.CompilerParams(collective_id=0, has_side_effects=True, vmem_limit_bytes=62 << 20),
        name="gather_logits_reduce",
    )(jnp.transpose(hidden, (1, 0, 2)), weight, targets, plan, row_grad)
    weight_grad, hidden_grad, logprob, scale = pl.pallas_call(
        hand_on_kernel,
        out_shape=outs,
        in_specs=[hbm] * 4,
        out_specs=(hbm,) * 4,
        scratch_shapes=[pltpu.VMEM(out.shape, out.dtype) for out in outs] + [dma((7,)), dma((7,))],
        compiler_params=pltpu.CompilerParams(vmem_limit_bytes=62 << 20),
        name="hand_on",
    )(*results)
    return logprob, jnp.transpose(hidden_grad, (1, 0, 2)), weight_grad, scale


def solution(mesh):
    placed = (P(None, None, "tensor"), P(("section", "tensor"), None), P(), P(), P())
    return jax.shard_map(
        per_device,
        mesh=mesh,
        in_specs=placed,
        out_specs=(P(), P(None, None, "tensor"), P(("section", "tensor"), None), P()),
        check_vma=False,
    )
```

```python
import functools

import jax
import jax.numpy as jnp
from jax import lax
from jax.experimental import pallas as pl
from jax.experimental.pallas import tpu as pltpu
from jax.sharding import PartitionSpec as P

MESH = pl.DeviceIdType.MESH
CAP = 30.0
F32 = jnp.float32
BF16 = jnp.bfloat16
MICRO = 4
ROWS = 52
SLOT = 64
V = 272
D = 4608
SH = 144
NEAR = (1, 7, 2, 6, 3, 5, 4)
FAR = (4, 3, 5, 2, 6, 1, 7)


def coords():
    s = lax.axis_index("section")
    t = lax.axis_index("tensor")
    x_hi, z = lax.rem(s, 2), lax.div(s, 2)
    q, y, c = lax.div(t, 16), lax.rem(lax.div(t, 2), 8), lax.rem(t, 2)
    return x_hi * 2 + q, y, z, c


def dev(x, y, z, c):
    x, y, z, c = lax.rem(x + 4, 4), lax.rem(y + 8, 8), lax.rem(z + 8, 8), lax.rem(c + 2, 2)
    return (z * 2 + lax.div(x, 2), lax.rem(x, 2) * 16 + y * 2 + c)


def rcopy(src, dst, ss, rs, to):
    return pltpu.make_async_remote_copy(
        src_ref=src, dst_ref=dst, send_sem=ss, recv_sem=rs, device_id=to, device_id_type=MESH
    )


def slot_lanes(ref, wide, plan_ref, fill, dtype):
    wide[...] = jnp.zeros_like(wide)
    wide[:, 0:ROWS] = ref[...]
    parts = []
    for k in range(MICRO):
        row = jnp.zeros((1, SLOT), dtype)
        for j in range(MICRO):
            row = jnp.where(plan_ref[k] == j, wide[j : j + 1, 0:SLOT], row)
        parts.append(row)
    flat = jnp.concatenate(parts, axis=1)
    lane = lax.broadcasted_iota(jnp.int32, (1, 4 * SLOT), 1)
    return jnp.where(lax.rem(lane, SLOT) < ROWS, flat, jnp.full_like(flat, fill))


def comm_kernel(
    hidden_ref, weight_ref, targets_ref, plan_ref, grad_ref,
    weight_grad_ref, hidden_grad_ref, logprob_ref, scale_ref,
    hid, tgt, grd, pln, tgt_wide, grd_wide, spread, pad, h, w, wt, wt_in, wg, term, term_in, hot, hot_in,
    own, xtx, xrx, ztx, zrx, own_t, xtx_t, xrx_t, ztx_t, zrx_t,
    ytx, yrx, rtx, rrx, atx, arx, tot_tx, tot_rx,
    in_sem, o_sem,
    gy_s, gy_r, gz_s, gz_r, gx_s, gx_r, gc_s, gc_r,
    t_s, t_r, w_s, w_r, m_s, m_r, x_s, x_r, z_s, z_r, xt_s, xt_r, zt_s, zt_r,
    y_s, y_r, r_s, r_r, a_s, a_r, b_s, b_r,
):
    x, y, z, c = coords()
    q, x_hi, p, zq = lax.rem(x, 2), lax.div(x, 2), lax.rem(z, 2), lax.div(z, 2)
    other = 1 - q
    first = p == 0
    me = q * 16 + y * 2 + c
    partner = dev(x, y, z, 1 - c)

    barrier = pltpu.get_barrier_semaphore()
    peers = [dev(x, y + d, z, c) for d in range(1, 8)]
    peers += [dev(x + a, y, z, c + b) for a in range(4) for b in range(2) if a or b]
    peers += [dev(x + 2 * a, y, z + d, c) for d in range(1, 8) for a in range(2)]
    loads = [
        pltpu.make_async_copy(src, dst, in_sem.at[i])
        for i, (src, dst) in enumerate(
            ((hidden_ref, hid), (plan_ref, pln), (targets_ref, tgt), (grad_ref, grd), (weight_ref, w))
        )
    ]
    for load in loads:
        load.start()
    for peer in peers:
        pl.semaphore_signal(barrier, inc=1, device_id=peer, device_id_type=MESH)

    pad[...] = jnp.zeros_like(pad)
    loads[0].wait()
    spread[...] = hid[...].astype(F32)
    for k in range(MICRO):
        pad[k * SLOT : k * SLOT + ROWS, 0:SH] = spread[:, k, :]
    mine = jnp.transpose(pad[...], (1, 0))[0:SH]
    h[0, me] = mine[:, 0:128].astype(BF16)
    h[1, me] = mine[:, 128:256].astype(BF16)
    pl.semaphore_wait(barrier, len(peers))

    def along(i):
        return 1 - 2 * lax.rem(i, 2)

    def shard(x_lo, yy):
        return x_lo * 16 + yy * 2 + c

    def y_copy(yy, to_y):
        t = shard(q, yy)
        return rcopy(h.at[p, t], h.at[p, t], gy_s.at[to_y], gy_r.at[yy], dev(x, to_y, z, c))

    def z_copy(yy, half):
        t = shard(q, yy)
        return rcopy(h.at[half, t], h.at[half, t], gz_s.at[yy], gz_r.at[yy], dev(x, y, z + along(yy), c))

    def x_copy(x_lo, yy, half):
        t = shard(x_lo, yy)
        return rcopy(h.at[half, t], h.at[half, t], gx_s.at[half, yy], gx_r.at[half, yy], dev(x + along(yy), y, z, c))

    def c_copy(x_lo, yy, cc, half):
        t = x_lo * 16 + yy * 2 + cc
        i = x_lo * 8 + yy
        return rcopy(h.at[half, t], h.at[half, t], gc_s.at[half, i], gc_r.at[half, i], partner)

    def rows_of(i, cc):
        return pl.ds(pl.multiple_of((i * 2 + cc) * SH, 16), SH)

    def w_copy(i):
        return rcopy(wt.at[rows_of(i, 1 - c)], wt_in.at[i], w_s.at[i], w_r.at[i], partner)

    term_copy = rcopy(term, term_in, m_s, m_r, partner)

    def to_x(half, yy, way):
        return rcopy(xtx.at[half, yy], xrx.at[half, yy], x_s.at[half, yy], x_r.at[half, yy], dev(x + way, y, z, c))

    def to_z(x_lo, yy):
        return rcopy(ztx.at[x_lo, yy], zrx.at[x_lo, yy], z_s.at[x_lo, yy], z_r.at[x_lo, yy], dev(x, y, z + along(yy), c))

    def to_x_t(yy):
        return rcopy(xtx_t.at[yy], xrx_t.at[yy], xt_s.at[yy], xt_r.at[yy], dev(x + along(yy), y, z, c))

    def to_z_t(x_lo, yy):
        return rcopy(ztx_t.at[x_lo, yy], zrx_t.at[x_lo, yy], zt_s.at[x_lo, yy], zt_r.at[x_lo, yy], dev(x, y, z + along(yy), c))

    def to_y(frm, to):
        return rcopy(ytx.at[to], yrx.at[frm], y_s.at[to], y_r.at[frm], dev(x, to, z, c))

    def at_y(d):
        return lax.rem(y + d, 8)

    def part_a(k):
        return lax.div(k, 2) * 4 + lax.rem(k, 2)

    def part_b(k):
        return part_a(k) + 2

    def halves(value):
        low, high = value[:, 0:128], value[:, 128:256]
        return jnp.where(first, low, high), jnp.where(first, high, low)

    def from_mine(i, ref):
        return jnp.dot(wt[rows_of(i, c), :], ref[...], preferred_element_type=F32)

    def from_theirs(i, ref):
        return jnp.dot(wt_in[i], ref[...], preferred_element_type=F32)

    for d in NEAR:
        y_copy(y, at_y(d)).start()
    for half in range(2):
        x_copy(q, y, half).start()
        c_copy(q, y, c, half).start()

    loads[4].wait()
    for j in range(D // 128):
        wt[j * 128 : (j + 1) * 128, :] = jnp.transpose(w[:, j * 128 : (j + 1) * 128], (1, 0))

    def start_w(i, _):
        w_copy(i).start()
        return 0

    lax.fori_loop(0, 16, start_w, 0)
    for load in loads[1:4]:
        load.wait()
    slot_target = slot_lanes(tgt, tgt_wide, pln, -1, jnp.int32)
    slot_grad = slot_lanes(grd, grd_wide, pln, 0.0, F32)
    s_id, t_id = lax.axis_index("section"), lax.axis_index("tensor")
    entry = lax.broadcasted_iota(jnp.int32, (V, 256), 0)
    hit = (s_id * 32 + t_id) * V + entry == slot_target
    hot[...] = hit.astype(F32).astype(BF16)
    hot_in[...] = ((s_id * 32 + t_id + 1 - 2 * c) * V + entry == slot_target).astype(F32).astype(BF16)

    def target_mine(i, _):
        own_t[i] = from_mine(i, hot).astype(BF16)
        return 0

    def target_rows(i, _):
        x_lo, yy = lax.div(i, 8), lax.rem(i, 8)
        w_copy(i).wait_recv()
        keep, pass_on = halves(own_t[i].astype(F32) + from_theirs(i, hot_in))
        own_t[i, :, 0:128] = keep.astype(BF16)
        ztx_t[x_lo, yy] = pass_on.astype(BF16)
        to_z_t(x_lo, yy).start()
        return 0

    for n, d in enumerate(NEAR):
        yy = at_y(d)
        y_copy(yy, y).wait_recv()
        z_copy(yy, p).start()
        x_copy(q, yy, p).start()
        c_copy(q, yy, c, p).start()
        if n < 4:
            lax.fori_loop(4 * n, 4 * n + 4, target_mine, 0)
    for n, d in enumerate(NEAR):
        yy = at_y(d)
        z_copy(yy, 1 - p).wait_recv()
        x_copy(q, yy, 1 - p).start()
        c_copy(q, yy, c, 1 - p).start()
        x_copy(other, yy, p).wait_recv()
        c_copy(other, yy, c, p).start()
        lax.fori_loop(2 * n, 2 * n + 2, target_rows, 0)
    x_copy(other, y, p).wait_recv()
    c_copy(other, y, c, p).start()
    for d in (0,) + NEAR:
        yy = at_y(d)
        x_copy(other, yy, 1 - p).wait_recv()
        c_copy(other, yy, c, 1 - p).start()
    lax.fori_loop(14, 16, target_rows, 0)

    def columns(b):
        return jnp.concatenate(
            [h[half, pl.ds(b * 8, 8)].reshape(8 * SH, 128) for half in range(2)], axis=1
        )

    def blocks(i, raw):
        b = lax.rem(q * 2 + i, 4)
        x_lo = lax.div(b, 2)
        for k in range(4):
            for half in range(2):
                c_copy(x_lo, lax.rem(b, 2) * 4 + k, 1 - c, half).wait_recv()
        part = w[:, pl.ds(pl.multiple_of(b * 8 * SH, 128), 8 * SH)]
        return raw + jnp.dot(part, columns(b), preferred_element_type=F32)

    raw = lax.fori_loop(0, 4, blocks, jnp.zeros((V, 256), F32))
    capped = CAP * jnp.tanh(raw / CAP)
    exponent = jnp.exp(capped)
    curve = 1.0 - jnp.square(capped / CAP)
    sums = jnp.concatenate(
        [
            jnp.sum(exponent, axis=0, keepdims=True),
            jnp.sum(jnp.where(hit, capped, 0.0), axis=0, keepdims=True),
        ],
        axis=0,
    )

    def member_of(stage, j):
        if stage == 0:
            return dev(lax.div(j, 2), y, z, lax.rem(j, 2))
        return dev(x, j, z, c) if stage == 1 else dev(x, y, j, c)

    index_of = (x * 2 + c, y, z)

    def tot_copy(stage, frm, d):
        to = member_of(stage, lax.rem(index_of[stage] + d, 8))
        return rcopy(tot_tx.at[stage], tot_rx.at[stage, frm], t_s.at[stage, d], t_r.at[stage, frm], to)

    def begin(stage, values):
        tot_tx[stage] = values
        tot_rx[stage, index_of[stage]] = values
        for d in FAR:
            tot_copy(stage, index_of[stage], d).start()

    def end(stage):
        for d in FAR:
            tot_copy(stage, lax.rem(index_of[stage] + d, 8), d).wait()
        total = tot_rx[stage, 0]
        for j in range(1, 8):
            total = total + tot_rx[stage, j]
        return total

    begin(0, sums)
    term[...] = jnp.where(hit, 0.0, exponent * curve).astype(BF16)
    term_copy.start()

    def mine_first(k, _):
        for i in (other * 8 + part_a(k), other * 8 + part_b(k), q * 8 + part_b(k)):
            own[i] = from_mine(i, term)
        return 0

    lax.fori_loop(0, 4, mine_first, 0)
    term_copy.wait_recv()

    def send_first(k, _):
        ya, yb = part_a(k), part_b(k)
        value = own[other * 8 + ya] + from_theirs(other * 8 + ya, term_in)
        for half in range(2):
            xtx[half, ya] = value[:, half * 128 : (half + 1) * 128].astype(BF16)
            to_x(half, ya, 1 - 2 * half).start()
        for x_lo in (other, q):
            i = x_lo * 8 + yb
            keep, pass_on = halves(own[i] + from_theirs(i, term_in))
            ztx[x_lo, yb] = pass_on.astype(BF16)
            to_z(x_lo, yb).start()
            own[i, :, 0:128] = keep
        return 0

    lax.fori_loop(0, 2, send_first, 0)
    begin(1, end(0))
    lax.fori_loop(2, 4, send_first, 0)

    def keep_first(k, _):
        i = q * 8 + part_a(k)
        own[i] = from_mine(i, term) + from_theirs(i, term_in)
        return 0

    lax.fori_loop(0, 4, keep_first, 0)

    def send_x_t(yy, _):
        to_z_t(other, yy).wait_recv()
        i = other * 8 + yy
        xtx_t[yy] = (own_t[i, :, 0:128].astype(F32) + zrx_t[other, yy].astype(F32)).astype(BF16)
        to_x_t(yy).start()
        return 0

    lax.fori_loop(0, 8, send_x_t, 0)

    def send_second(k, _):
        ya, yb = part_a(k), part_b(k)
        to_z(other, yb).wait_recv()
        xtx[0, yb] = (own[other * 8 + yb, :, 0:128] + zrx[other, yb].astype(F32)).astype(BF16)
        to_x(0, yb, along(yb)).start()
        i = q * 8 + ya
        both = own[i]
        for half in range(2):
            to_x(half, ya, 1 - 2 * half).wait_recv()
        both = both + jnp.concatenate([xrx[0, ya], xrx[1, ya]], axis=1).astype(F32)
        keep, pass_on = halves(both)
        ztx[0, ya] = pass_on.astype(BF16)
        to_z(0, ya).start()
        own[i, :, 0:128] = keep
        return 0

    lax.fori_loop(0, 2, send_second, 0)
    begin(2, end(1))
    lax.fori_loop(2, 4, send_second, 0)

    def ready_a(k, _):
        i, yy = q * 8 + part_a(k), part_a(k)
        to_z(0, yy).wait_recv()
        own[i, :, 0:128] = own[i, :, 0:128] + zrx[0, yy].astype(F32)
        return 0

    def ready_b(k, _):
        i, yy = q * 8 + part_b(k), part_b(k)
        to_z(q, yy).wait_recv()
        to_x(0, yy, along(yy)).wait_recv()
        own[i, :, 0:128] = own[i, :, 0:128] + zrx[q, yy].astype(F32) + xrx[0, yy].astype(F32)
        return 0

    def ready_t(yy, _):
        i = q * 8 + yy
        to_z_t(q, yy).wait_recv()
        to_x_t(yy).wait_recv()
        own_t[i, :, 0:128] = (own_t[i, :, 0:128].astype(F32) + zrx_t[q, yy].astype(F32) + xrx_t[yy].astype(F32)).astype(BF16)
        return 0

    lax.fori_loop(0, 8, ready_t, 0)
    lax.fori_loop(0, 4, ready_a, 0)
    lax.fori_loop(0, 4, ready_b, 0)
    sums = end(2)
    total, target_logit = sums[0:1], sums[1:2]
    target_curve = 1.0 - jnp.square(target_logit / CAP)
    coef_t = slot_grad * (1.0 - jnp.exp(target_logit) / total) * target_curve
    coef_s = slot_grad / total
    half_t = jnp.where(first, coef_t[:, 0:128], coef_t[:, 128:256])
    half_s = jnp.where(first, coef_s[:, 0:128], coef_s[:, 128:256])

    def merged(yy):
        i = q * 8 + yy
        return half_t * own_t[i, :, 0:128].astype(F32) - half_s * own[i, :, 0:128]

    def send_y(k, _):
        yy = lax.rem(y + k, 8)
        ytx[yy] = merged(yy).astype(BF16)
        to_y(y, yy).start()
        return 0

    lax.fori_loop(1, 8, send_y, 0)
    acc = merged(y)

    soft = (-(slot_grad * (exponent / total)) * curve).astype(BF16)

    def grad_block(b, _):
        wg[:, pl.ds(pl.multiple_of(b * 8 * SH, 128), 8 * SH)] = lax.dot_general(
            soft, columns(b), (((1,), (1,)), ((), ())), preferred_element_type=F32
        ).astype(BF16)
        return 0

    lax.fori_loop(0, 4, grad_block, 0)
    wg_copy = pltpu.make_async_copy(wg, weight_grad_ref, o_sem)
    wg_copy.start()
    logprob = target_logit - jnp.log(total)
    scale = slot_grad * target_curve
    for m in range(MICRO):
        for value, out in ((logprob, logprob_ref), (scale, scale_ref)):
            row = jnp.zeros((1, ROWS), F32)
            for k in range(MICRO):
                row = jnp.where(pln[k] == m, value[:, k * SLOT : k * SLOT + ROWS], row)
            out[m : m + 1, :] = row

    for d in NEAR:
        yy = at_y(d)
        to_y(yy, y).wait_recv()
        acc = acc + yrx[yy].astype(F32)

    def member(j):
        return dev(2 * lax.rem(j, 2) + q, y, 2 * lax.div(j, 2) + p, c)

    index = zq * 2 + x_hi
    for j in range(8):
        rtx[j, 0:16] = acc[16 * j : 16 * j + 16].astype(BF16)
        rtx[j, 16:32] = acc[128:144].astype(BF16)

    def to_member(frm, to):
        return rcopy(rtx.at[to], rrx.at[frm], r_s.at[to], r_r.at[frm], member(to))

    for d in FAR:
        to_member(index, lax.rem(index + d, 8)).start()
    rrx[index] = rtx[index]
    for d in FAR:
        to_member(lax.rem(index + d, 8), index).wait_recv()
    done = rrx[0].astype(F32)
    for j in range(1, 8):
        done = done + rrx[j].astype(F32)
    atx[...] = done.astype(BF16)

    z2 = z + 1 - 2 * p
    slot = pl.ds(pl.multiple_of(index * 16, 16), 16)
    tail = pl.ds(128, 16)
    arx[p, slot] = atx[0:16]
    arx[p, tail] = atx[16:32]
    tail_copy = rcopy(atx.at[pl.ds(16, 16)], arx.at[p, tail], b_s, b_r, dev(x, y, z2, c))
    tail_copy.start()
    mates = [(a, d) for d in FAR + (0,) for a in range(2) if a or d]

    def to_mate(n, a, d):
        return rcopy(atx.at[pl.ds(0, 16)], arx.at[p, slot], a_s.at[n], a_r.at[n], dev(x + 2 * a, y, z + d, c))

    def from_mate(n, a, d):
        zz = lax.rem(z - d + 8, 8)
        pp = lax.rem(zz, 2)
        ii = lax.div(zz, 2) * 2 + lax.rem(x_hi + a, 2)
        there = pl.ds(pl.multiple_of(ii * 16, 16), 16)
        return rcopy(atx.at[pl.ds(0, 16)], arx.at[pp, there], a_s.at[n], a_r.at[n], dev(x + 2 * a, y, z - d, c))

    for n, (a, d) in enumerate(mates):
        to_mate(n, a, d).start()

    for d in FAR:
        y_copy(y, at_y(d)).wait_send()
    for d in NEAR:
        z_copy(at_y(d), p).wait_send()
    for d in (0,) + NEAR:
        for half in range(2):
            x_copy(q, at_y(d), half).wait_send()
            for x_lo in range(2):
                c_copy(x_lo, at_y(d), c, half).wait_send()
    term_copy.wait_send()

    def drain(yy, _):
        to_x_t(yy).wait_send()
        for x_lo in range(2):
            w_copy(x_lo * 8 + yy).wait_send()
            to_z_t(x_lo, yy).wait_send()
        return 0

    def drain_ab(k, _):
        ya, yb = part_a(k), part_b(k)
        for half in range(2):
            to_x(half, ya, 1 - 2 * half).wait_send()
            to_z(half, yb).wait_send()
        to_z(0, ya).wait_send()
        to_x(0, yb, along(yb)).wait_send()
        return 0

    lax.fori_loop(0, 8, drain, 0)
    lax.fori_loop(0, 4, drain_ab, 0)
    for d in FAR:
        to_y(y, at_y(d)).wait_send()
        to_member(index, lax.rem(index + d, 8)).wait_send()
    wg_copy.wait()
    for n, (a, d) in enumerate(mates):
        from_mate(n, a, d).wait_recv()
        to_mate(n, a, d).wait_send()
    rcopy(atx.at[pl.ds(16, 16)], arx.at[1 - p, tail], b_s, b_r, dev(x, y, z2, c)).wait()
    for half in range(2):
        wide = jnp.concatenate([arx[half].astype(F32), jnp.zeros((256 - SH, 128), F32)], axis=0)
        flat = jnp.transpose(wide, (1, 0))
        for k in range(2):
            spread[:, half * 2 + k, :] = flat[k * SLOT : k * SLOT + ROWS, 0:SH]
    hidden_grad_ref[...] = spread[...].astype(BF16)


def hand_on_kernel(a0, a1, a2, a3, b0, b1, b2, b3, v0, v1, v2, v3, sem_in, sem_out):
    cuts = [(0, 64), (64, 64), (128, 64), (192, 80)]
    pieces = [(a0.at[pl.ds(i, n)], v0.at[pl.ds(i, n)], b0.at[pl.ds(i, n)]) for i, n in cuts]
    pieces += [(a1, v1, b1), (a2, v2, b2), (a3, v3, b3)]
    reads = [pltpu.make_async_copy(a, v, sem_in.at[i]) for i, (a, v, b) in enumerate(pieces)]
    writes = [pltpu.make_async_copy(v, b, sem_out.at[i]) for i, (a, v, b) in enumerate(pieces)]
    for read in reads:
        read.start()
    for read, write in zip(reads, writes):
        read.wait()
        write.start()
    for write in writes:
        write.wait()


def per_device(hidden, weight, targets, plan, row_grad):
    vmem = pl.BlockSpec(memory_space=pltpu.VMEM)
    hbm = pl.BlockSpec(memory_space=pl.ANY)
    dma = pltpu.SemaphoreType.DMA
    piece = (SH, 128)
    outs = (
        jax.ShapeDtypeStruct((V, D), BF16),
        jax.ShapeDtypeStruct((ROWS, MICRO, SH), BF16),
        jax.ShapeDtypeStruct((MICRO, ROWS), F32),
        jax.ShapeDtypeStruct((MICRO, ROWS), F32),
    )
    def buf(*shape, dtype=BF16):
        return pltpu.VMEM(shape, dtype)

    results = pl.pallas_call(
        comm_kernel,
        out_shape=outs,
        in_specs=[hbm] * 5,
        out_specs=(hbm, vmem, vmem, vmem),
        scratch_shapes=[
            buf(ROWS, MICRO, SH), buf(MICRO, ROWS, dtype=jnp.int32), buf(MICRO, ROWS, dtype=F32),
            pltpu.SMEM((MICRO,), jnp.int32),
            buf(MICRO, 128, dtype=jnp.int32), buf(MICRO, 128, dtype=F32),
            buf(ROWS, MICRO, SH, dtype=F32), buf(256, 256, dtype=F32),
            buf(2, 32, *piece), buf(V, D), buf(D, V), buf(16, SH, V), buf(V, D),
            buf(V, 256), buf(V, 256), buf(V, 256), buf(V, 256),
            buf(16, SH, 256, dtype=F32), buf(2, 8, *piece), buf(2, 8, *piece), buf(2, 8, *piece), buf(2, 8, *piece),
            buf(16, SH, 256), buf(8, *piece), buf(8, *piece), buf(2, 8, *piece), buf(2, 8, *piece),
            buf(8, *piece), buf(8, *piece), buf(8, 32, 128), buf(8, 32, 128), buf(32, 128), buf(2, *piece),
            buf(3, 2, 256, dtype=F32), buf(3, 8, 2, 256, dtype=F32),
            dma((5,)), dma,
            dma((8,)), dma((8,)), dma((8,)), dma((8,)), dma((2, 8)), dma((2, 8)), dma((2, 16)), dma((2, 16)),
            dma((3, 8)), dma((3, 8)), dma((16,)), dma((16,)), dma, dma,
            dma((2, 8)), dma((2, 8)), dma((2, 8)), dma((2, 8)), dma((8,)), dma((8,)), dma((2, 8)), dma((2, 8)),
            dma((8,)), dma((8,)), dma((8,)), dma((8,)), dma((15,)), dma((15,)), dma, dma,
        ],
        compiler_params=pltpu.CompilerParams(collective_id=0, has_side_effects=True, vmem_limit_bytes=62 << 20),
        name="gather_logits_reduce",
    )(jnp.transpose(hidden, (1, 0, 2)), weight, targets, plan, row_grad)
    weight_grad, hidden_grad, logprob, scale = pl.pallas_call(
        hand_on_kernel,
        out_shape=outs,
        in_specs=[hbm] * 4,
        out_specs=(hbm,) * 4,
        scratch_shapes=[pltpu.VMEM(out.shape, out.dtype) for out in outs] + [dma((7,)), dma((7,))],
        compiler_params=pltpu.CompilerParams(vmem_limit_bytes=62 << 20),
        name="hand_on",
    )(*results)
    return logprob, jnp.transpose(hidden_grad, (1, 0, 2)), weight_grad, scale


def solution(mesh):
    placed = (P(None, None, "tensor"), P(("section", "tensor"), None), P(), P(), P())
    return jax.shard_map(
        per_device,
        mesh=mesh,
        in_specs=placed,
        out_specs=(P(), P(None, None, "tensor"), P(("section", "tensor"), None), P()),
        check_vma=False,
    )
```

```python
import functools

import jax
import jax.numpy as jnp
from jax import lax
from jax.experimental import pallas as pl
from jax.experimental.pallas import tpu as pltpu
from jax.sharding import PartitionSpec as P

MESH = pl.DeviceIdType.MESH
CAP = 30.0
F32 = jnp.float32
BF16 = jnp.bfloat16
MICRO = 4
ROWS = 52
SLOT = 64
V = 272
D = 4608
SH = 144
PART = 80
NEAR = (1, 7, 2, 6, 3, 5, 4)
FAR = (4, 3, 5, 2, 6, 1, 7)


def coords():
    s = lax.axis_index("section")
    t = lax.axis_index("tensor")
    x_hi, z = lax.rem(s, 2), lax.div(s, 2)
    q, y, c = lax.div(t, 16), lax.rem(lax.div(t, 2), 8), lax.rem(t, 2)
    return x_hi * 2 + q, y, z, c


def dev(x, y, z, c):
    x, y, z, c = lax.rem(x + 4, 4), lax.rem(y + 8, 8), lax.rem(z + 8, 8), lax.rem(c + 2, 2)
    return (z * 2 + lax.div(x, 2), lax.rem(x, 2) * 16 + y * 2 + c)


def rcopy(src, dst, ss, rs, to):
    return pltpu.make_async_remote_copy(
        src_ref=src, dst_ref=dst, send_sem=ss, recv_sem=rs, device_id=to, device_id_type=MESH
    )


def slot_lanes(ref, wide, plan_ref, fill, dtype):
    wide[...] = jnp.zeros_like(wide)
    wide[:, 0:ROWS] = ref[...]
    parts = []
    for k in range(MICRO):
        row = jnp.zeros((1, SLOT), dtype)
        for j in range(MICRO):
            row = jnp.where(plan_ref[k] == j, wide[j : j + 1, 0:SLOT], row)
        parts.append(row)
    flat = jnp.concatenate(parts, axis=1)
    lane = lax.broadcasted_iota(jnp.int32, (1, 4 * SLOT), 1)
    return jnp.where(lax.rem(lane, SLOT) < ROWS, flat, jnp.full_like(flat, fill))


def comm_kernel(
    hidden_ref, weight_ref, targets_ref, plan_ref, grad_ref,
    weight_grad_ref, hidden_grad_ref, logprob_ref, scale_ref,
    hid, tgt, grd, pln, tgt_wide, grd_wide, spread, pad, h, w, wt, wt_in, wg, term, term_in, hot, hot_in,
    own, xtx, xrx, ztx, zrx, own_t, xtx_t, xrx_t, ztx_t, zrx_t,
    ytx, yrx, atx, arx, tot_tx, tot_rx,
    in_sem, o_sem,
    gy_s, gy_r, gz_s, gz_r, gx_s, gx_r, gxz_s, gc_s, gc_r,
    t_s, t_r, w_s, w_r, m_s, m_r, x_s, x_r, z_s, z_r, xt_s, xt_r, zt_s, zt_r,
    y_s, y_r, a_s, a_r,
):
    x, y, z, c = coords()
    q, x_hi, p, zq = lax.rem(x, 2), lax.div(x, 2), lax.rem(z, 2), lax.div(z, 2)
    other = 1 - q
    first = p == 0
    me = q * 16 + y * 2 + c
    partner = dev(x, y, z, 1 - c)

    barrier = pltpu.get_barrier_semaphore()
    peers = [dev(x, y + d, z, c) for d in range(1, 8)]
    peers += [dev(x + a, y, z, c + b) for a in range(4) for b in range(2) if a or b]
    peers += [dev(x + 2 * a, y, z + d, c) for d in range(1, 8) for a in range(2)]
    peers += [dev(x + d, y, z + d, c) for d in (1, -1)]
    peers += [dev(x + 2, y + d, z, c) for d in range(1, 8)]
    loads = [
        pltpu.make_async_copy(src, dst, in_sem.at[i])
        for i, (src, dst) in enumerate(
            ((hidden_ref, hid), (plan_ref, pln), (targets_ref, tgt), (grad_ref, grd), (weight_ref, w))
        )
    ]
    for load in loads:
        load.start()
    for peer in peers:
        pl.semaphore_signal(barrier, inc=1, device_id=peer, device_id_type=MESH)

    pad[...] = jnp.zeros_like(pad)
    loads[0].wait()
    spread[...] = hid[...].astype(F32)
    for k in range(MICRO):
        pad[k * SLOT : k * SLOT + ROWS, 0:SH] = spread[:, k, :]
    mine = jnp.transpose(pad[...], (1, 0))[0:SH]
    h[0, me] = mine[:, 0:128].astype(BF16)
    h[1, me] = mine[:, 128:256].astype(BF16)
    pl.semaphore_wait(barrier, len(peers))

    def along(i):
        return 1 - 2 * lax.rem(i, 2)

    def shard(x_lo, yy):
        return x_lo * 16 + yy * 2 + c

    def y_copy(yy, to_y):
        t = shard(q, yy)
        return rcopy(h.at[p, t], h.at[p, t], gy_s.at[to_y], gy_r.at[yy], dev(x, to_y, z, c))

    def z_copy(yy, half):
        t = shard(q, yy)
        return rcopy(h.at[half, t], h.at[half, t], gz_s.at[yy], gz_r.at[yy], dev(x, y, z + along(yy), c))

    def x_copy(x_lo, yy, half):
        t = shard(x_lo, yy)
        return rcopy(h.at[half, t], h.at[half, t], gx_s.at[half, yy], gx_r.at[half, yy], dev(x + along(yy), y, z, c))

    def xz_copy(x_lo, yy, half):
        t = shard(x_lo, yy)
        to = dev(x + along(yy), y, z + along(yy), c)
        return rcopy(h.at[half, t], h.at[half, t], gxz_s.at[yy], gx_r.at[half, yy], to)

    def c_copy(x_lo, yy, cc, half):
        t = x_lo * 16 + yy * 2 + cc
        i = x_lo * 8 + yy
        return rcopy(h.at[half, t], h.at[half, t], gc_s.at[half, i], gc_r.at[half, i], partner)

    def rows_of(i, cc):
        return pl.ds(pl.multiple_of((i * 2 + cc) * SH, 16), SH)

    def w_copy(i):
        return rcopy(wt.at[rows_of(i, 1 - c)], wt_in.at[i], w_s.at[i], w_r.at[i], partner)

    term_copy = rcopy(term, term_in, m_s, m_r, partner)

    def to_x(half, yy, way):
        return rcopy(xtx.at[half, yy], xrx.at[half, yy], x_s.at[half, yy], x_r.at[half, yy], dev(x + way, y, z, c))

    def to_z(x_lo, yy):
        return rcopy(ztx.at[x_lo, yy], zrx.at[x_lo, yy], z_s.at[x_lo, yy], z_r.at[x_lo, yy], dev(x, y, z + along(yy), c))

    def to_x_t(yy):
        return rcopy(xtx_t.at[yy], xrx_t.at[yy], xt_s.at[yy], xt_r.at[yy], dev(x + along(yy), y, z, c))

    def to_z_t(x_lo, yy):
        return rcopy(ztx_t.at[x_lo, yy], zrx_t.at[x_lo, yy], zt_s.at[x_lo, yy], zt_r.at[x_lo, yy], dev(x, y, z + along(yy), c))

    def to_y(frm, to, a):
        rows = pl.ds(pl.multiple_of(64 * lax.rem(x_hi + a, 2), 16), PART)
        return rcopy(ytx.at[to, rows], yrx.at[x_hi, frm], y_s.at[a, to], y_r.at[x_hi, frm], dev(x + 2 * a, to, z, c))

    def from_y(frm, a):
        other_hi = lax.rem(x_hi + a, 2)
        return rcopy(ytx.at[0, pl.ds(0, PART)], yrx.at[other_hi, frm], y_s.at[a, frm], y_r.at[other_hi, frm], dev(x + 2 * a, frm, z, c))

    def at_y(d):
        return lax.rem(y + d, 8)

    def part_a(k):
        return lax.div(k, 2) * 4 + lax.rem(k, 2)

    def part_b(k):
        return part_a(k) + 2

    def halves(value):
        low, high = value[:, 0:128], value[:, 128:256]
        return jnp.where(first, low, high), jnp.where(first, high, low)

    def from_mine(i, ref):
        return jnp.dot(wt[rows_of(i, c), :], ref[...], preferred_element_type=F32)

    def from_theirs(i, ref):
        return jnp.dot(wt_in[i], ref[...], preferred_element_type=F32)

    for d in NEAR:
        y_copy(y, at_y(d)).start()
    for half in range(2):
        x_copy(q, y, half).start()
        c_copy(q, y, c, half).start()

    loads[4].wait()
    for j in range(D // 128):
        wt[j * 128 : (j + 1) * 128, :] = jnp.transpose(w[:, j * 128 : (j + 1) * 128], (1, 0))

    def start_w(i, _):
        w_copy(i).start()
        return 0

    lax.fori_loop(0, 16, start_w, 0)
    for load in loads[1:4]:
        load.wait()
    slot_target = slot_lanes(tgt, tgt_wide, pln, -1, jnp.int32)
    slot_grad = slot_lanes(grd, grd_wide, pln, 0.0, F32)
    s_id, t_id = lax.axis_index("section"), lax.axis_index("tensor")
    entry = lax.broadcasted_iota(jnp.int32, (V, 256), 0)
    hit = (s_id * 32 + t_id) * V + entry == slot_target
    hot[...] = hit.astype(F32).astype(BF16)
    hot_in[...] = ((s_id * 32 + t_id + 1 - 2 * c) * V + entry == slot_target).astype(F32).astype(BF16)

    def target_rows(i, _):
        i = lax.rem(other * 8 + i, 16)
        x_lo, yy = lax.div(i, 8), lax.rem(i, 8)
        w_copy(i).wait_recv()
        keep, pass_on = halves(from_mine(i, hot) + from_theirs(i, hot_in))
        own_t[i] = keep.astype(BF16)
        ztx_t[x_lo, yy] = pass_on.astype(BF16)
        to_z_t(x_lo, yy).start()
        return 0

    for d in NEAR:
        yy = at_y(d)
        y_copy(yy, y).wait_recv()
        x_copy(q, yy, p).start()
        xz_copy(q, yy, p).start()
        z_copy(yy, p).start()
        c_copy(q, yy, c, p).start()
    for n, d in enumerate(NEAR):
        yy = at_y(d)
        z_copy(yy, 1 - p).wait_recv()
        c_copy(q, yy, c, 1 - p).start()
        x_copy(other, yy, p).wait_recv()
        c_copy(other, yy, c, p).start()
        lax.fori_loop(2 * n, 2 * n + 2, target_rows, 0)
    x_copy(other, y, p).wait_recv()
    c_copy(other, y, c, p).start()
    for d in (0,) + NEAR:
        yy = at_y(d)
        x_copy(other, yy, 1 - p).wait_recv()
        c_copy(other, yy, c, 1 - p).start()
    lax.fori_loop(14, 16, target_rows, 0)

    def send_x_t(yy, _):
        to_z_t(other, yy).wait_recv()
        i = other * 8 + yy
        xtx_t[yy] = own_t[i] + zrx_t[other, yy]
        to_x_t(yy).start()
        return 0

    lax.fori_loop(0, 8, send_x_t, 0)

    def columns(b):
        return jnp.concatenate(
            [h[half, pl.ds(b * 8, 8)].reshape(8 * SH, 128) for half in range(2)], axis=1
        )

    def blocks(i, raw):
        b = lax.rem(q * 2 + i, 4)
        x_lo = lax.div(b, 2)
        for k in range(4):
            for half in range(2):
                c_copy(x_lo, lax.rem(b, 2) * 4 + k, 1 - c, half).wait_recv()
        part = w[:, pl.ds(pl.multiple_of(b * 8 * SH, 128), 8 * SH)]
        return raw + jnp.dot(part, columns(b), preferred_element_type=F32)

    raw = lax.fori_loop(0, 4, blocks, jnp.zeros((V, 256), F32))
    capped = CAP * jnp.tanh(raw / CAP)
    exponent = jnp.exp(capped)
    curve = 1.0 - jnp.square(capped / CAP)
    sums = jnp.concatenate(
        [
            jnp.sum(exponent, axis=0, keepdims=True),
            jnp.sum(jnp.where(hit, capped, 0.0), axis=0, keepdims=True),
        ],
        axis=0,
    )

    def member_of(stage, j):
        if stage == 0:
            return dev(lax.div(j, 2), y, z, lax.rem(j, 2))
        return dev(x, j, z, c) if stage == 1 else dev(x, y, j, c)

    index_of = (x * 2 + c, y, z)

    def tot_copy(stage, frm, d):
        to = member_of(stage, lax.rem(index_of[stage] + d, 8))
        return rcopy(tot_tx.at[stage], tot_rx.at[stage, frm], t_s.at[stage, d], t_r.at[stage, frm], to)

    def begin(stage, values):
        tot_tx[stage] = values
        tot_rx[stage, index_of[stage]] = values
        for d in FAR:
            tot_copy(stage, index_of[stage], d).start()

    def end(stage):
        for d in FAR:
            tot_copy(stage, lax.rem(index_of[stage] + d, 8), d).wait()
        total = tot_rx[stage, 0]
        for j in range(1, 8):
            total = total + tot_rx[stage, j]
        return total

    begin(0, sums)
    term[...] = jnp.where(hit, 0.0, exponent * curve).astype(BF16)
    term_copy.start()

    def mine_first(k, _):
        for i in (other * 8 + part_a(k), other * 8 + part_b(k), q * 8 + part_b(k)):
            own[i] = from_mine(i, term)
        return 0

    lax.fori_loop(0, 4, mine_first, 0)
    term_copy.wait_recv()

    def send_first(k, _):
        ya, yb = part_a(k), part_b(k)
        value = own[other * 8 + ya] + from_theirs(other * 8 + ya, term_in)
        for half in range(2):
            xtx[half, ya] = value[:, half * 128 : (half + 1) * 128].astype(BF16)
            to_x(half, ya, 1 - 2 * half).start()
        for x_lo in (other, q):
            i = x_lo * 8 + yb
            keep, pass_on = halves(own[i] + from_theirs(i, term_in))
            ztx[x_lo, yb] = pass_on.astype(BF16)
            to_z(x_lo, yb).start()
            own[i, :, 0:128] = keep
        return 0

    lax.fori_loop(0, 2, send_first, 0)
    begin(1, end(0))
    lax.fori_loop(2, 4, send_first, 0)

    def keep_first(k, _):
        i = q * 8 + part_a(k)
        own[i] = from_mine(i, term) + from_theirs(i, term_in)
        return 0

    lax.fori_loop(0, 4, keep_first, 0)

    def send_second(k, _):
        ya, yb = part_a(k), part_b(k)
        to_z(other, yb).wait_recv()
        xtx[0, yb] = (own[other * 8 + yb, :, 0:128] + zrx[other, yb].astype(F32)).astype(BF16)
        to_x(0, yb, along(yb)).start()
        i = q * 8 + ya
        both = own[i]
        for half in range(2):
            to_x(half, ya, 1 - 2 * half).wait_recv()
        both = both + jnp.concatenate([xrx[0, ya], xrx[1, ya]], axis=1).astype(F32)
        keep, pass_on = halves(both)
        ztx[0, ya] = pass_on.astype(BF16)
        to_z(0, ya).start()
        own[i, :, 0:128] = keep
        return 0

    lax.fori_loop(0, 2, send_second, 0)
    begin(2, end(1))
    lax.fori_loop(2, 4, send_second, 0)

    def ready_a(k, _):
        i, yy = q * 8 + part_a(k), part_a(k)
        to_z(0, yy).wait_recv()
        own[i, :, 0:128] = own[i, :, 0:128] + zrx[0, yy].astype(F32)
        return 0

    def ready_b(k, _):
        i, yy = q * 8 + part_b(k), part_b(k)
        to_z(q, yy).wait_recv()
        to_x(0, yy, along(yy)).wait_recv()
        own[i, :, 0:128] = own[i, :, 0:128] + zrx[q, yy].astype(F32) + xrx[0, yy].astype(F32)
        return 0

    def ready_t(yy, _):
        i = q * 8 + yy
        to_z_t(q, yy).wait_recv()
        to_x_t(yy).wait_recv()
        own_t[i] = own_t[i] + zrx_t[q, yy] + xrx_t[yy]
        return 0

    lax.fori_loop(0, 8, ready_t, 0)
    lax.fori_loop(0, 4, ready_a, 0)
    lax.fori_loop(0, 4, ready_b, 0)
    sums = end(2)
    total, target_logit = sums[0:1], sums[1:2]
    target_curve = 1.0 - jnp.square(target_logit / CAP)
    coef_t = slot_grad * (1.0 - jnp.exp(target_logit) / total) * target_curve
    coef_s = slot_grad / total
    half_t = jnp.where(first, coef_t[:, 0:128], coef_t[:, 128:256])
    half_s = jnp.where(first, coef_s[:, 0:128], coef_s[:, 128:256])

    def merged(yy):
        i = q * 8 + yy
        return half_t * own_t[i].astype(F32) - half_s * own[i, :, 0:128]

    def send_y(k, _):
        yy = lax.rem(y + k, 8)
        ytx[yy] = merged(yy).astype(BF16)
        to_y(y, yy, 0).start()
        to_y(y, yy, 1).start()
        return 0

    lax.fori_loop(1, 8, send_y, 0)
    mine = merged(y)
    ytx[y] = mine.astype(BF16)
    to_y(y, y, 1).start()
    own[q * 8 + y, :, 0:128] = mine
    acc = own[q * 8 + y, pl.ds(pl.multiple_of(64 * x_hi, 16), PART), 0:128]

    soft = (-(slot_grad * (exponent / total)) * curve).astype(BF16)

    def grad_block(b, _):
        wg[:, pl.ds(pl.multiple_of(b * 8 * SH, 128), 8 * SH)] = lax.dot_general(
            soft, columns(b), (((1,), (1,)), ((), ())), preferred_element_type=F32
        ).astype(BF16)
        return 0

    lax.fori_loop(0, 4, grad_block, 0)
    wg_copy = pltpu.make_async_copy(wg, weight_grad_ref, o_sem)
    wg_copy.start()
    logprob = target_logit - jnp.log(total)
    scale = slot_grad * target_curve
    for m in range(MICRO):
        for value, out in ((logprob, logprob_ref), (scale, scale_ref)):
            row = jnp.zeros((1, ROWS), F32)
            for k in range(MICRO):
                row = jnp.where(pln[k] == m, value[:, k * SLOT : k * SLOT + ROWS], row)
            out[m : m + 1, :] = row

    for d in NEAR:
        yy = at_y(d)
        for a in range(2):
            from_y(yy, a).wait_recv()
            acc = acc + yrx[lax.rem(x_hi + a, 2), yy].astype(F32)
    from_y(y, 1).wait_recv()
    acc = acc + yrx[1 - x_hi, y].astype(F32)

    atx[...] = acc.astype(BF16)
    arx[x_hi, z] = atx[...]
    mates = [(a, d) for d in FAR + (0,) for a in range(2) if a or d]

    def to_mate(n, a, d):
        return rcopy(atx, arx.at[x_hi, z], a_s.at[n], a_r.at[n], dev(x + 2 * a, y, z + d, c))

    def from_mate(n, a, d):
        there = arx.at[lax.rem(x_hi + a, 2), lax.rem(z - d + 8, 8)]
        return rcopy(atx, there, a_s.at[n], a_r.at[n], dev(x + 2 * a, y, z - d, c))

    for n, (a, d) in enumerate(mates):
        to_mate(n, a, d).start()

    for d in FAR:
        y_copy(y, at_y(d)).wait_send()
    for d in NEAR:
        z_copy(at_y(d), p).wait_send()
        x_copy(q, at_y(d), p).wait_send()
        xz_copy(q, at_y(d), p).wait_send()
    for d in (0,) + NEAR:
        for half in range(2):
            for x_lo in range(2):
                c_copy(x_lo, at_y(d), c, half).wait_send()
    for half in range(2):
        x_copy(q, y, half).wait_send()
    term_copy.wait_send()

    def drain(yy, _):
        to_x_t(yy).wait_send()
        for x_lo in range(2):
            w_copy(x_lo * 8 + yy).wait_send()
            to_z_t(x_lo, yy).wait_send()
        return 0

    def drain_ab(k, _):
        ya, yb = part_a(k), part_b(k)
        for half in range(2):
            to_x(half, ya, 1 - 2 * half).wait_send()
            to_z(half, yb).wait_send()
        to_z(0, ya).wait_send()
        to_x(0, yb, along(yb)).wait_send()
        return 0

    lax.fori_loop(0, 8, drain, 0)
    lax.fori_loop(0, 4, drain_ab, 0)
    for d in FAR:
        for a in range(2):
            to_y(y, at_y(d), a).wait_send()
    to_y(y, y, 1).wait_send()
    wg_copy.wait()
    for n, (a, d) in enumerate(mates):
        from_mate(n, a, d).wait_recv()
        to_mate(n, a, d).wait_send()
    for half in range(2):
        parts = []
        for hi in range(2):
            part = arx[hi, half].astype(F32)
            for k in range(1, 4):
                part = part + arx[hi, 2 * k + half].astype(F32)
            parts.append(part)
        wide = jnp.concatenate([parts[0], parts[1][2 * PART - SH :], jnp.zeros((256 - SH, 128), F32)], axis=0)
        flat = jnp.transpose(wide, (1, 0))
        for k in range(2):
            spread[:, half * 2 + k, :] = flat[k * SLOT : k * SLOT + ROWS, 0:SH]
    hidden_grad_ref[...] = spread[...].astype(BF16)


def hand_on_kernel(a0, a1, a2, a3, b0, b1, b2, b3, v0, v1, v2, v3, sem_in, sem_out):
    cuts = [(0, 64), (64, 64), (128, 64), (192, 80)]
    pieces = [(a0.at[pl.ds(i, n)], v0.at[pl.ds(i, n)], b0.at[pl.ds(i, n)]) for i, n in cuts]
    pieces += [(a1, v1, b1), (a2, v2, b2), (a3, v3, b3)]
    reads = [pltpu.make_async_copy(a, v, sem_in.at[i]) for i, (a, v, b) in enumerate(pieces)]
    writes = [pltpu.make_async_copy(v, b, sem_out.at[i]) for i, (a, v, b) in enumerate(pieces)]
    for read in reads:
        read.start()
    for read, write in zip(reads, writes):
        read.wait()
        write.start()
    for write in writes:
        write.wait()


def per_device(hidden, weight, targets, plan, row_grad):
    vmem = pl.BlockSpec(memory_space=pltpu.VMEM)
    hbm = pl.BlockSpec(memory_space=pl.ANY)
    dma = pltpu.SemaphoreType.DMA
    piece = (SH, 128)
    outs = (
        jax.ShapeDtypeStruct((V, D), BF16),
        jax.ShapeDtypeStruct((ROWS, MICRO, SH), BF16),
        jax.ShapeDtypeStruct((MICRO, ROWS), F32),
        jax.ShapeDtypeStruct((MICRO, ROWS), F32),
    )
    def buf(*shape, dtype=BF16):
        return pltpu.VMEM(shape, dtype)

    results = pl.pallas_call(
        comm_kernel,
        out_shape=outs,
        in_specs=[hbm] * 5,
        out_specs=(hbm, vmem, vmem, vmem),
        scratch_shapes=[
            buf(ROWS, MICRO, SH), buf(MICRO, ROWS, dtype=jnp.int32), buf(MICRO, ROWS, dtype=F32),
            pltpu.SMEM((MICRO,), jnp.int32),
            buf(MICRO, 128, dtype=jnp.int32), buf(MICRO, 128, dtype=F32),
            buf(ROWS, MICRO, SH, dtype=F32), buf(256, 256, dtype=F32),
            buf(2, 32, *piece), buf(V, D), buf(D, V), buf(16, SH, V), buf(V, D),
            buf(V, 256), buf(V, 256), buf(V, 256), buf(V, 256),
            buf(16, SH, 256, dtype=F32), buf(2, 8, *piece), buf(2, 8, *piece), buf(2, 8, *piece), buf(2, 8, *piece),
            buf(16, *piece), buf(8, *piece), buf(8, *piece), buf(2, 8, *piece), buf(2, 8, *piece),
            buf(8, *piece), buf(2, 8, PART, 128), buf(PART, 128), buf(2, 8, PART, 128),
            buf(3, 2, 256, dtype=F32), buf(3, 8, 2, 256, dtype=F32),
            dma((5,)), dma,
            dma((8,)), dma((8,)), dma((8,)), dma((8,)), dma((2, 8)), dma((2, 8)), dma((8,)), dma((2, 16)), dma((2, 16)),
            dma((3, 8)), dma((3, 8)), dma((16,)), dma((16,)), dma, dma,
            dma((2, 8)), dma((2, 8)), dma((2, 8)), dma((2, 8)), dma((8,)), dma((8,)), dma((2, 8)), dma((2, 8)),
            dma((2, 8)), dma((2, 8)), dma((15,)), dma((15,)),
        ],
        compiler_params=pltpu.CompilerParams(collective_id=0, has_side_effects=True, vmem_limit_bytes=62 << 20),
        name="gather_logits_reduce",
    )(jnp.transpose(hidden, (1, 0, 2)), weight, targets, plan, row_grad)
    weight_grad, hidden_grad, logprob, scale = pl.pallas_call(
        hand_on_kernel,
        out_shape=outs,
        in_specs=[hbm] * 4,
        out_specs=(hbm,) * 4,
        scratch_shapes=[pltpu.VMEM(out.shape, out.dtype) for out in outs] + [dma((7,)), dma((7,))],
        compiler_params=pltpu.CompilerParams(vmem_limit_bytes=62 << 20),
        name="hand_on",
    )(*results)
    return logprob, jnp.transpose(hidden_grad, (1, 0, 2)), weight_grad, scale


def solution(mesh):
    placed = (P(None, None, "tensor"), P(("section", "tensor"), None), P(), P(), P())
    return jax.shard_map(
        per_device,
        mesh=mesh,
        in_specs=placed,
        out_specs=(P(), P(None, None, "tensor"), P(("section", "tensor"), None), P()),
        check_vma=False,
    )
```

```python
import functools

import jax
import jax.numpy as jnp
from jax import lax
from jax.experimental import pallas as pl
from jax.experimental.pallas import tpu as pltpu
from jax.sharding import PartitionSpec as P

MESH = pl.DeviceIdType.MESH
CAP = 30.0
F32 = jnp.float32
BF16 = jnp.bfloat16
MICRO = 4
ROWS = 52
SLOT = 64
V = 272
D = 4608
SH = 144
PART = 80
NEAR = (1, 7, 2, 6, 3, 5, 4)
FAR = (4, 3, 5, 2, 6, 1, 7)


def coords():
    s = lax.axis_index("section")
    t = lax.axis_index("tensor")
    x_hi, z = lax.rem(s, 2), lax.div(s, 2)
    q, y, c = lax.div(t, 16), lax.rem(lax.div(t, 2), 8), lax.rem(t, 2)
    return x_hi * 2 + q, y, z, c


def dev(x, y, z, c):
    x, y, z, c = lax.rem(x + 4, 4), lax.rem(y + 8, 8), lax.rem(z + 8, 8), lax.rem(c + 2, 2)
    return (z * 2 + lax.div(x, 2), lax.rem(x, 2) * 16 + y * 2 + c)


def rcopy(src, dst, ss, rs, to):
    return pltpu.make_async_remote_copy(
        src_ref=src, dst_ref=dst, send_sem=ss, recv_sem=rs, device_id=to, device_id_type=MESH
    )


def slot_lanes(ref, wide, plan_ref, fill, dtype):
    wide[...] = jnp.zeros_like(wide)
    wide[:, 0:ROWS] = ref[...]
    parts = []
    for k in range(MICRO):
        row = jnp.zeros((1, SLOT), dtype)
        for j in range(MICRO):
            row = jnp.where(plan_ref[k] == j, wide[j : j + 1, 0:SLOT], row)
        parts.append(row)
    flat = jnp.concatenate(parts, axis=1)
    lane = lax.broadcasted_iota(jnp.int32, (1, 4 * SLOT), 1)
    return jnp.where(lax.rem(lane, SLOT) < ROWS, flat, jnp.full_like(flat, fill))


def comm_kernel(
    hidden_ref, weight_ref, targets_ref, plan_ref, grad_ref,
    weight_grad_ref, hidden_grad_ref, logprob_ref, scale_ref,
    hid, tgt, grd, pln, tgt_wide, grd_wide, spread, pad, h, w, wt, wt_in, wg, term, term_in, hot, hot_in,
    own, xtx, xrx, ztx, zrx, own_t, xtx_t, xrx_t, ztx_t, zrx_t,
    ytx, yrx, atx, arx, tot_tx, tot_rx,
    in_sem, o_sem,
    gy_s, gy_r, gz_s, gz_r, gx_s, gx_r, gxz_s, gc_s, gc_r,
    t_s, t_r, w_s, w_r, m_s, m_r, x_s, x_r, z_s, z_r, xt_s, xt_r, zt_s, zt_r,
    y_s, y_r, a_s, a_r,
):
    x, y, z, c = coords()
    q, x_hi, p, zq = lax.rem(x, 2), lax.div(x, 2), lax.rem(z, 2), lax.div(z, 2)
    other = 1 - q
    first = p == 0
    me = q * 16 + y * 2 + c
    partner = dev(x, y, z, 1 - c)

    barrier = pltpu.get_barrier_semaphore()
    peers = [dev(x, y + d, z, c) for d in range(1, 8)]
    peers += [dev(x + a, y, z, c + b) for a in range(4) for b in range(2) if a or b]
    peers += [dev(x + 2 * a, y, z + d, c) for d in range(1, 8) for a in range(2)]
    peers += [dev(x + d, y, z + d, c) for d in (1, -1)]
    peers += [dev(x + 2, y + d, z, c) for d in range(1, 8)]
    loads = [
        pltpu.make_async_copy(src, dst, in_sem.at[i])
        for i, (src, dst) in enumerate(
            ((hidden_ref, hid), (plan_ref, pln), (targets_ref, tgt), (grad_ref, grd), (weight_ref, w))
        )
    ]
    for load in loads:
        load.start()
    for peer in peers:
        pl.semaphore_signal(barrier, inc=1, device_id=peer, device_id_type=MESH)

    pad[...] = jnp.zeros_like(pad)
    loads[0].wait()
    spread[...] = hid[...].astype(F32)
    for k in range(MICRO):
        pad[k * SLOT : k * SLOT + ROWS, 0:SH] = spread[:, k, :]
    mine = jnp.transpose(pad[...], (1, 0))[0:SH]
    h[0, me] = mine[:, 0:128].astype(BF16)
    h[1, me] = mine[:, 128:256].astype(BF16)
    pl.semaphore_wait(barrier, len(peers))

    def along(i):
        return 1 - 2 * lax.rem(i, 2)

    def shard(x_lo, yy):
        return x_lo * 16 + yy * 2 + c

    def y_copy(yy, to_y):
        t = shard(q, yy)
        return rcopy(h.at[p, t], h.at[p, t], gy_s.at[to_y], gy_r.at[yy], dev(x, to_y, z, c))

    def z_copy(yy, half):
        t = shard(q, yy)
        return rcopy(h.at[half, t], h.at[half, t], gz_s.at[yy], gz_r.at[yy], dev(x, y, z + along(yy), c))

    def x_copy(x_lo, yy, half):
        t = shard(x_lo, yy)
        return rcopy(h.at[half, t], h.at[half, t], gx_s.at[half, yy], gx_r.at[half, yy], dev(x + along(yy), y, z, c))

    def xz_copy(x_lo, yy, half):
        t = shard(x_lo, yy)
        to = dev(x + along(yy), y, z + along(yy), c)
        return rcopy(h.at[half, t], h.at[half, t], gxz_s.at[yy], gx_r.at[half, yy], to)

    def c_copy(x_lo, yy, cc, half):
        t = x_lo * 16 + yy * 2 + cc
        i = x_lo * 8 + yy
        return rcopy(h.at[half, t], h.at[half, t], gc_s.at[half, i], gc_r.at[half, i], partner)

    def rows_of(i, cc):
        return pl.ds(pl.multiple_of((i * 2 + cc) * SH, 16), SH)

    def w_copy(i):
        return rcopy(wt.at[rows_of(i, 1 - c)], wt_in.at[i], w_s.at[i], w_r.at[i], partner)

    term_copy = rcopy(term, term_in, m_s, m_r, partner)

    def to_x(half, yy, way):
        return rcopy(xtx.at[half, yy], xrx.at[half, yy], x_s.at[half, yy], x_r.at[half, yy], dev(x + way, y, z, c))

    def to_z(x_lo, yy):
        return rcopy(ztx.at[x_lo, yy], zrx.at[x_lo, yy], z_s.at[x_lo, yy], z_r.at[x_lo, yy], dev(x, y, z + along(yy), c))

    def to_x_t(half, yy, way):
        return rcopy(xtx_t.at[half, yy], xrx_t.at[half, yy], xt_s.at[half, yy], xt_r.at[half, yy], dev(x + way, y, z, c))

    def to_z_t(x_lo, yy):
        return rcopy(ztx_t.at[x_lo, yy], zrx_t.at[x_lo, yy], zt_s.at[x_lo, yy], zt_r.at[x_lo, yy], dev(x, y, z + along(yy), c))

    def to_y(frm, to, a):
        rows = pl.ds(pl.multiple_of(64 * lax.rem(x_hi + a, 2), 16), PART)
        return rcopy(ytx.at[to, rows], yrx.at[x_hi, frm], y_s.at[a, to], y_r.at[x_hi, frm], dev(x + 2 * a, to, z, c))

    def from_y(frm, a):
        other_hi = lax.rem(x_hi + a, 2)
        return rcopy(ytx.at[0, pl.ds(0, PART)], yrx.at[other_hi, frm], y_s.at[a, frm], y_r.at[other_hi, frm], dev(x + 2 * a, frm, z, c))

    def at_y(d):
        return lax.rem(y + d, 8)

    def part_a(k):
        return lax.div(k, 2) * 4 + lax.rem(k, 2)

    def part_b(k):
        return part_a(k) + 2

    def halves(value):
        low, high = value[:, 0:128], value[:, 128:256]
        return jnp.where(first, low, high), jnp.where(first, high, low)

    def from_mine(i, ref):
        return jnp.dot(wt[rows_of(i, c), :], ref[...], preferred_element_type=F32)

    def from_theirs(i, ref):
        return jnp.dot(wt_in[i], ref[...], preferred_element_type=F32)

    for d in NEAR:
        y_copy(y, at_y(d)).start()
    for half in range(2):
        x_copy(q, y, half).start()
        c_copy(q, y, c, half).start()

    loads[4].wait()
    for j in range(D // 128):
        wt[j * 128 : (j + 1) * 128, :] = jnp.transpose(w[:, j * 128 : (j + 1) * 128], (1, 0))

    def start_w(i, _):
        w_copy(i).start()
        return 0

    lax.fori_loop(0, 16, start_w, 0)
    for load in loads[1:4]:
        load.wait()
    slot_target = slot_lanes(tgt, tgt_wide, pln, -1, jnp.int32)
    slot_grad = slot_lanes(grd, grd_wide, pln, 0.0, F32)
    s_id, t_id = lax.axis_index("section"), lax.axis_index("tensor")
    entry = lax.broadcasted_iota(jnp.int32, (V, 256), 0)
    hit = (s_id * 32 + t_id) * V + entry == slot_target
    hot[...] = hit.astype(F32).astype(BF16)
    hot_in[...] = ((s_id * 32 + t_id + 1 - 2 * c) * V + entry == slot_target).astype(F32).astype(BF16)

    def target_rows(i):
        w_copy(i).wait_recv()
        return from_mine(i, hot) + from_theirs(i, hot_in)

    def target_first(k, _):
        ya, yb = part_a(k), part_b(k)
        value = target_rows(other * 8 + ya).astype(BF16)
        for half in range(2):
            xtx_t[half, ya] = value[:, half * 128 : (half + 1) * 128]
            to_x_t(half, ya, 1 - 2 * half).start()
        for x_lo in (other, q):
            i = x_lo * 8 + yb
            keep, pass_on = halves(target_rows(i))
            ztx_t[x_lo, yb] = pass_on.astype(BF16)
            to_z_t(x_lo, yb).start()
            own_t[i, :, 0:128] = keep.astype(BF16)
        return 0

    def target_keep(k, _):
        i = q * 8 + part_a(k)
        own_t[i] = target_rows(i).astype(BF16)
        return 0

    for d in NEAR:
        yy = at_y(d)
        y_copy(yy, y).wait_recv()
        x_copy(q, yy, p).start()
        xz_copy(q, yy, p).start()
        z_copy(yy, p).start()
        c_copy(q, yy, c, p).start()
    for n, d in enumerate(NEAR):
        yy = at_y(d)
        z_copy(yy, 1 - p).wait_recv()
        c_copy(q, yy, c, 1 - p).start()
        x_copy(other, yy, p).wait_recv()
        c_copy(other, yy, c, p).start()
        if n < 4:
            target_first(n, 0)
        elif n < 6:
            lax.fori_loop(2 * n - 8, 2 * n - 6, target_keep, 0)
    x_copy(other, y, p).wait_recv()
    c_copy(other, y, c, p).start()
    for d in (0,) + NEAR:
        yy = at_y(d)
        x_copy(other, yy, 1 - p).wait_recv()
        c_copy(other, yy, c, 1 - p).start()

    def target_second(k, _):
        ya, yb = part_a(k), part_b(k)
        to_z_t(other, yb).wait_recv()
        xtx_t[0, yb] = own_t[other * 8 + yb, :, 0:128] + zrx_t[other, yb]
        to_x_t(0, yb, along(yb)).start()
        i = q * 8 + ya
        for half in range(2):
            to_x_t(half, ya, 1 - 2 * half).wait_recv()
        both = own_t[i] + jnp.concatenate([xrx_t[0, ya], xrx_t[1, ya]], axis=1)
        keep, pass_on = halves(both.astype(F32))
        ztx_t[0, ya] = pass_on.astype(BF16)
        to_z_t(0, ya).start()
        own_t[i, :, 0:128] = keep.astype(BF16)
        return 0


    def columns(b):
        return jnp.concatenate(
            [h[half, pl.ds(b * 8, 8)].reshape(8 * SH, 128) for half in range(2)], axis=1
        )

    def blocks(i, raw):
        b = lax.rem(q * 2 + i, 4)
        x_lo = lax.div(b, 2)
        for k in range(4):
            for half in range(2):
                c_copy(x_lo, lax.rem(b, 2) * 4 + k, 1 - c, half).wait_recv()
        part = w[:, pl.ds(pl.multiple_of(b * 8 * SH, 128), 8 * SH)]
        return raw + jnp.dot(part, columns(b), preferred_element_type=F32)

    raw = lax.fori_loop(0, 4, blocks, jnp.zeros((V, 256), F32))
    capped = CAP * jnp.tanh(raw / CAP)
    exponent = jnp.exp(capped)
    curve = 1.0 - jnp.square(capped / CAP)
    sums = jnp.concatenate(
        [
            jnp.sum(exponent, axis=0, keepdims=True),
            jnp.sum(jnp.where(hit, capped, 0.0), axis=0, keepdims=True),
        ],
        axis=0,
    )

    def member_of(stage, j):
        if stage == 0:
            return dev(lax.div(j, 2), y, z, lax.rem(j, 2))
        return dev(x, j, z, c) if stage == 1 else dev(x, y, j, c)

    index_of = (x * 2 + c, y, z)

    def tot_copy(stage, frm, d):
        to = member_of(stage, lax.rem(index_of[stage] + d, 8))
        return rcopy(tot_tx.at[stage], tot_rx.at[stage, frm], t_s.at[stage, d], t_r.at[stage, frm], to)

    def begin(stage, values):
        tot_tx[stage] = values
        tot_rx[stage, index_of[stage]] = values
        for d in FAR:
            tot_copy(stage, index_of[stage], d).start()

    def end(stage):
        for d in FAR:
            tot_copy(stage, lax.rem(index_of[stage] + d, 8), d).wait()
        total = tot_rx[stage, 0]
        for j in range(1, 8):
            total = total + tot_rx[stage, j]
        return total

    begin(0, sums)
    term[...] = jnp.where(hit, 0.0, exponent * curve).astype(BF16)
    term_copy.start()

    def mine_first(k, _):
        for i in (other * 8 + part_a(k), other * 8 + part_b(k), q * 8 + part_b(k)):
            own[i] = from_mine(i, term)
        return 0

    lax.fori_loop(0, 4, mine_first, 0)
    lax.fori_loop(0, 4, target_second, 0)
    term_copy.wait_recv()

    def send_first(k, _):
        ya, yb = part_a(k), part_b(k)
        value = own[other * 8 + ya] + from_theirs(other * 8 + ya, term_in)
        for half in range(2):
            xtx[half, ya] = value[:, half * 128 : (half + 1) * 128].astype(BF16)
            to_x(half, ya, 1 - 2 * half).start()
        for x_lo in (other, q):
            i = x_lo * 8 + yb
            keep, pass_on = halves(own[i] + from_theirs(i, term_in))
            ztx[x_lo, yb] = pass_on.astype(BF16)
            to_z(x_lo, yb).start()
            own[i, :, 0:128] = keep
        return 0

    lax.fori_loop(0, 2, send_first, 0)
    begin(1, end(0))
    lax.fori_loop(2, 4, send_first, 0)

    def keep_first(k, _):
        i = q * 8 + part_a(k)
        own[i] = from_mine(i, term) + from_theirs(i, term_in)
        return 0

    lax.fori_loop(0, 4, keep_first, 0)

    def send_second(k, _):
        ya, yb = part_a(k), part_b(k)
        to_z(other, yb).wait_recv()
        xtx[0, yb] = (own[other * 8 + yb, :, 0:128] + zrx[other, yb].astype(F32)).astype(BF16)
        to_x(0, yb, along(yb)).start()
        i = q * 8 + ya
        both = own[i]
        for half in range(2):
            to_x(half, ya, 1 - 2 * half).wait_recv()
        both = both + jnp.concatenate([xrx[0, ya], xrx[1, ya]], axis=1).astype(F32)
        keep, pass_on = halves(both)
        ztx[0, ya] = pass_on.astype(BF16)
        to_z(0, ya).start()
        own[i, :, 0:128] = keep
        return 0

    lax.fori_loop(0, 2, send_second, 0)
    begin(2, end(1))
    lax.fori_loop(2, 4, send_second, 0)

    def ready_a(k, _):
        i, yy = q * 8 + part_a(k), part_a(k)
        to_z(0, yy).wait_recv()
        own[i, :, 0:128] = own[i, :, 0:128] + zrx[0, yy].astype(F32)
        return 0

    def ready_b(k, _):
        i, yy = q * 8 + part_b(k), part_b(k)
        to_z(q, yy).wait_recv()
        to_x(0, yy, along(yy)).wait_recv()
        own[i, :, 0:128] = own[i, :, 0:128] + zrx[q, yy].astype(F32) + xrx[0, yy].astype(F32)
        return 0

    def ready_t(k, _):
        i, yy = q * 8 + part_a(k), part_a(k)
        to_z_t(0, yy).wait_recv()
        own_t[i, :, 0:128] = own_t[i, :, 0:128] + zrx_t[0, yy]
        i, yy = q * 8 + part_b(k), part_b(k)
        to_z_t(q, yy).wait_recv()
        to_x_t(0, yy, along(yy)).wait_recv()
        own_t[i, :, 0:128] = own_t[i, :, 0:128] + zrx_t[q, yy] + xrx_t[0, yy]
        return 0

    lax.fori_loop(0, 4, ready_t, 0)
    lax.fori_loop(0, 4, ready_a, 0)
    lax.fori_loop(0, 4, ready_b, 0)
    sums = end(2)
    total, target_logit = sums[0:1], sums[1:2]
    target_curve = 1.0 - jnp.square(target_logit / CAP)
    coef_t = slot_grad * (1.0 - jnp.exp(target_logit) / total) * target_curve
    coef_s = slot_grad / total
    half_t = jnp.where(first, coef_t[:, 0:128], coef_t[:, 128:256])
    half_s = jnp.where(first, coef_s[:, 0:128], coef_s[:, 128:256])

    def merged(yy):
        i = q * 8 + yy
        return half_t * own_t[i, :, 0:128].astype(F32) - half_s * own[i, :, 0:128]

    def send_y(k, _):
        yy = lax.rem(y + k, 8)
        ytx[yy] = merged(yy).astype(BF16)
        to_y(y, yy, 0).start()
        to_y(y, yy, 1).start()
        return 0

    lax.fori_loop(1, 8, send_y, 0)
    mine = merged(y)
    ytx[y] = mine.astype(BF16)
    to_y(y, y, 1).start()
    own[q * 8 + y, :, 0:128] = mine
    acc = own[q * 8 + y, pl.ds(pl.multiple_of(64 * x_hi, 16), PART), 0:128]

    soft = (-(slot_grad * (exponent / total)) * curve).astype(BF16)

    def grad_block(b, _):
        wg[:, pl.ds(pl.multiple_of(b * 8 * SH, 128), 8 * SH)] = lax.dot_general(
            soft, columns(b), (((1,), (1,)), ((), ())), preferred_element_type=F32
        ).astype(BF16)
        return 0

    lax.fori_loop(0, 4, grad_block, 0)
    wg_copy = pltpu.make_async_copy(wg, weight_grad_ref, o_sem)
    wg_copy.start()
    logprob = target_logit - jnp.log(total)
    scale = slot_grad * target_curve
    for m in range(MICRO):
        for value, out in ((logprob, logprob_ref), (scale, scale_ref)):
            row = jnp.zeros((1, ROWS), F32)
            for k in range(MICRO):
                row = jnp.where(pln[k] == m, value[:, k * SLOT : k * SLOT + ROWS], row)
            out[m : m + 1, :] = row

    for d in NEAR:
        yy = at_y(d)
        for a in range(2):
            from_y(yy, a).wait_recv()
            acc = acc + yrx[lax.rem(x_hi + a, 2), yy].astype(F32)
    from_y(y, 1).wait_recv()
    acc = acc + yrx[1 - x_hi, y].astype(F32)

    atx[...] = acc.astype(BF16)
    arx[x_hi, z] = atx[...]
    mates = [(a, d) for d in FAR + (0,) for a in range(2) if a or d]

    def to_mate(n, a, d):
        return rcopy(atx, arx.at[x_hi, z], a_s.at[n], a_r.at[n], dev(x + 2 * a, y, z + d, c))

    def from_mate(n, a, d):
        there = arx.at[lax.rem(x_hi + a, 2), lax.rem(z - d + 8, 8)]
        return rcopy(atx, there, a_s.at[n], a_r.at[n], dev(x + 2 * a, y, z - d, c))

    for n, (a, d) in enumerate(mates):
        to_mate(n, a, d).start()

    for d in FAR:
        y_copy(y, at_y(d)).wait_send()
    for d in NEAR:
        z_copy(at_y(d), p).wait_send()
        x_copy(q, at_y(d), p).wait_send()
        xz_copy(q, at_y(d), p).wait_send()
    for d in (0,) + NEAR:
        for half in range(2):
            for x_lo in range(2):
                c_copy(x_lo, at_y(d), c, half).wait_send()
    for half in range(2):
        x_copy(q, y, half).wait_send()
    term_copy.wait_send()

    def drain(yy, _):
        for x_lo in range(2):
            w_copy(x_lo * 8 + yy).wait_send()
        return 0

    def drain_ab(k, _):
        ya, yb = part_a(k), part_b(k)
        for half in range(2):
            to_x(half, ya, 1 - 2 * half).wait_send()
            to_z(half, yb).wait_send()
            to_x_t(half, ya, 1 - 2 * half).wait_send()
            to_z_t(half, yb).wait_send()
        to_z(0, ya).wait_send()
        to_x(0, yb, along(yb)).wait_send()
        to_z_t(0, ya).wait_send()
        to_x_t(0, yb, along(yb)).wait_send()
        return 0

    lax.fori_loop(0, 8, drain, 0)
    lax.fori_loop(0, 4, drain_ab, 0)
    for d in FAR:
        for a in range(2):
            to_y(y, at_y(d), a).wait_send()
    to_y(y, y, 1).wait_send()
    wg_copy.wait()
    for n, (a, d) in enumerate(mates):
        from_mate(n, a, d).wait_recv()
        to_mate(n, a, d).wait_send()
    for half in range(2):
        parts = []
        for hi in range(2):
            part = arx[hi, half].astype(F32)
            for k in range(1, 4):
                part = part + arx[hi, 2 * k + half].astype(F32)
            parts.append(part)
        wide = jnp.concatenate([parts[0], parts[1][2 * PART - SH :], jnp.zeros((256 - SH, 128), F32)], axis=0)
        flat = jnp.transpose(wide, (1, 0))
        for k in range(2):
            spread[:, half * 2 + k, :] = flat[k * SLOT : k * SLOT + ROWS, 0:SH]
    hidden_grad_ref[...] = spread[...].astype(BF16)


def hand_on_kernel(a0, a1, a2, a3, b0, b1, b2, b3, v0, v1, v2, v3, sem_in, sem_out):
    cuts = [(0, 64), (64, 64), (128, 64), (192, 80)]
    pieces = [(a0.at[pl.ds(i, n)], v0.at[pl.ds(i, n)], b0.at[pl.ds(i, n)]) for i, n in cuts]
    pieces += [(a1, v1, b1), (a2, v2, b2), (a3, v3, b3)]
    reads = [pltpu.make_async_copy(a, v, sem_in.at[i]) for i, (a, v, b) in enumerate(pieces)]
    writes = [pltpu.make_async_copy(v, b, sem_out.at[i]) for i, (a, v, b) in enumerate(pieces)]
    for read in reads:
        read.start()
    for read, write in zip(reads, writes):
        read.wait()
        write.start()
    for write in writes:
        write.wait()


def per_device(hidden, weight, targets, plan, row_grad):
    vmem = pl.BlockSpec(memory_space=pltpu.VMEM)
    hbm = pl.BlockSpec(memory_space=pl.ANY)
    dma = pltpu.SemaphoreType.DMA
    piece = (SH, 128)
    outs = (
        jax.ShapeDtypeStruct((V, D), BF16),
        jax.ShapeDtypeStruct((ROWS, MICRO, SH), BF16),
        jax.ShapeDtypeStruct((MICRO, ROWS), F32),
        jax.ShapeDtypeStruct((MICRO, ROWS), F32),
    )
    def buf(*shape, dtype=BF16):
        return pltpu.VMEM(shape, dtype)

    results = pl.pallas_call(
        comm_kernel,
        out_shape=outs,
        in_specs=[hbm] * 5,
        out_specs=(hbm, vmem, vmem, vmem),
        scratch_shapes=[
            buf(ROWS, MICRO, SH), buf(MICRO, ROWS, dtype=jnp.int32), buf(MICRO, ROWS, dtype=F32),
            pltpu.SMEM((MICRO,), jnp.int32),
            buf(MICRO, 128, dtype=jnp.int32), buf(MICRO, 128, dtype=F32),
            buf(ROWS, MICRO, SH, dtype=F32), buf(256, 256, dtype=F32),
            buf(2, 32, *piece), buf(V, D), buf(D, V), buf(16, SH, V), buf(V, D),
            buf(V, 256), buf(V, 256), buf(V, 256), buf(V, 256),
            buf(16, SH, 256, dtype=F32), buf(2, 8, *piece), buf(2, 8, *piece), buf(2, 8, *piece), buf(2, 8, *piece),
            buf(16, SH, 256), buf(2, 8, *piece), buf(2, 8, *piece), buf(2, 8, *piece), buf(2, 8, *piece),
            buf(8, *piece), buf(2, 8, PART, 128), buf(PART, 128), buf(2, 8, PART, 128),
            buf(3, 2, 256, dtype=F32), buf(3, 8, 2, 256, dtype=F32),
            dma((5,)), dma,
            dma((8,)), dma((8,)), dma((8,)), dma((8,)), dma((2, 8)), dma((2, 8)), dma((8,)), dma((2, 16)), dma((2, 16)),
            dma((3, 8)), dma((3, 8)), dma((16,)), dma((16,)), dma, dma,
            dma((2, 8)), dma((2, 8)), dma((2, 8)), dma((2, 8)), dma((2, 8)), dma((2, 8)), dma((2, 8)), dma((2, 8)),
            dma((2, 8)), dma((2, 8)), dma((15,)), dma((15,)),
        ],
        compiler_params=pltpu.CompilerParams(collective_id=0, has_side_effects=True, vmem_limit_bytes=62 << 20),
        name="gather_logits_reduce",
    )(jnp.transpose(hidden, (1, 0, 2)), weight, targets, plan, row_grad)
    weight_grad, hidden_grad, logprob, scale = pl.pallas_call(
        hand_on_kernel,
        out_shape=outs,
        in_specs=[hbm] * 4,
        out_specs=(hbm,) * 4,
        scratch_shapes=[pltpu.VMEM(out.shape, out.dtype) for out in outs] + [dma((7,)), dma((7,))],
        compiler_params=pltpu.CompilerParams(vmem_limit_bytes=62 << 20),
        name="hand_on",
    )(*results)
    return logprob, jnp.transpose(hidden_grad, (1, 0, 2)), weight_grad, scale


def solution(mesh):
    placed = (P(None, None, "tensor"), P(("section", "tensor"), None), P(), P(), P())
    return jax.shard_map(
        per_device,
        mesh=mesh,
        in_specs=placed,
        out_specs=(P(), P(None, None, "tensor"), P(("section", "tensor"), None), P()),
        check_vma=False,
    )
```

```python
import functools

import jax
import jax.numpy as jnp
from jax import lax
from jax.experimental import pallas as pl
from jax.experimental.pallas import tpu as pltpu
from jax.sharding import PartitionSpec as P

MESH = pl.DeviceIdType.MESH
CAP = 30.0
F32 = jnp.float32
BF16 = jnp.bfloat16
MICRO = 4
ROWS = 52
SLOT = 64
V = 272
D = 4608
SH = 144
PART = 80
NEAR = (1, 7, 2, 6, 3, 5, 4)
FAR = (4, 3, 5, 2, 6, 1, 7)


def coords():
    s = lax.axis_index("section")
    t = lax.axis_index("tensor")
    x_hi, z = lax.rem(s, 2), lax.div(s, 2)
    q, y, c = lax.div(t, 16), lax.rem(lax.div(t, 2), 8), lax.rem(t, 2)
    return x_hi * 2 + q, y, z, c


def dev(x, y, z, c):
    x, y, z, c = lax.rem(x + 4, 4), lax.rem(y + 8, 8), lax.rem(z + 8, 8), lax.rem(c + 2, 2)
    return (z * 2 + lax.div(x, 2), lax.rem(x, 2) * 16 + y * 2 + c)


def rcopy(src, dst, ss, rs, to):
    return pltpu.make_async_remote_copy(
        src_ref=src, dst_ref=dst, send_sem=ss, recv_sem=rs, device_id=to, device_id_type=MESH
    )


def slot_lanes(ref, wide, plan_ref, fill, dtype):
    wide[...] = jnp.zeros_like(wide)
    wide[:, 0:ROWS] = ref[...]
    parts = []
    for k in range(MICRO):
        row = jnp.zeros((1, SLOT), dtype)
        for j in range(MICRO):
            row = jnp.where(plan_ref[k] == j, wide[j : j + 1, 0:SLOT], row)
        parts.append(row)
    flat = jnp.concatenate(parts, axis=1)
    lane = lax.broadcasted_iota(jnp.int32, (1, 4 * SLOT), 1)
    return jnp.where(lax.rem(lane, SLOT) < ROWS, flat, jnp.full_like(flat, fill))


def comm_kernel(
    hidden_ref, weight_ref, targets_ref, plan_ref, grad_ref,
    weight_grad_ref, hidden_grad_ref, logprob_ref, scale_ref,
    hid, tgt, grd, pln, tgt_wide, grd_wide, spread, pad, h, w, wt, wt_in, wg, term, term_in, hot, hot_in,
    own, xtx, xrx, ztx, zrx, own_t, xtx_t, xrx_t, ztx_t, zrx_t,
    ytx, yrx, atx, arx, tot_tx, tot_rx,
    in_sem, o_sem,
    gy_s, gy_r, gz_s, gz_r, gx_s, gx_r, gxz_s, gc_s, gc_r,
    t_s, t_r, w_s, w_r, m_s, m_r, x_s, x_r, z_s, z_r, xt_s, xt_r, zt_s, zt_r,
    y_s, y_r, a_s, a_r,
):
    x, y, z, c = coords()
    q, x_hi, p, zq = lax.rem(x, 2), lax.div(x, 2), lax.rem(z, 2), lax.div(z, 2)
    other = 1 - q
    first = p == 0
    me = q * 16 + y * 2 + c
    partner = dev(x, y, z, 1 - c)

    barrier = pltpu.get_barrier_semaphore()
    peers = [dev(x, y + d, z, c) for d in range(1, 8)]
    peers += [dev(x + a, y, z, c + b) for a in range(4) for b in range(2) if a or b]
    peers += [dev(x + 2 * a, y, z + d, c) for d in range(1, 8) for a in range(2)]
    peers += [dev(x + d, y, z + d, c) for d in (1, -1)]
    peers += [dev(x + 2, y + d, z, c) for d in range(1, 8)]
    loads = [
        pltpu.make_async_copy(src, dst, in_sem.at[i])
        for i, (src, dst) in enumerate(
            ((hidden_ref, hid), (plan_ref, pln), (targets_ref, tgt), (grad_ref, grd), (weight_ref, w))
        )
    ]
    for load in loads:
        load.start()
    for peer in peers:
        pl.semaphore_signal(barrier, inc=1, device_id=peer, device_id_type=MESH)

    pad[...] = jnp.zeros_like(pad)
    loads[0].wait()
    spread[...] = hid[...].astype(F32)
    for k in range(MICRO):
        pad[k * SLOT : k * SLOT + ROWS, 0:SH] = spread[:, k, :]
    mine = jnp.transpose(pad[...], (1, 0))[0:SH]
    h[0, me] = mine[:, 0:128].astype(BF16)
    h[1, me] = mine[:, 128:256].astype(BF16)
    pl.semaphore_wait(barrier, len(peers))

    def along(i):
        return 1 - 2 * lax.rem(i, 2)

    def shard(x_lo, yy):
        return x_lo * 16 + yy * 2 + c

    def y_copy(yy, to_y):
        t = shard(q, yy)
        return rcopy(h.at[p, t], h.at[p, t], gy_s.at[to_y], gy_r.at[yy], dev(x, to_y, z, c))

    def z_copy(yy, half):
        t = shard(q, yy)
        return rcopy(h.at[half, t], h.at[half, t], gz_s.at[yy], gz_r.at[yy], dev(x, y, z + along(yy), c))

    def x_copy(x_lo, yy, half):
        t = shard(x_lo, yy)
        return rcopy(h.at[half, t], h.at[half, t], gx_s.at[half, yy], gx_r.at[half, yy], dev(x + along(yy), y, z, c))

    def xz_copy(x_lo, yy, half):
        t = shard(x_lo, yy)
        to = dev(x + along(yy), y, z + along(yy), c)
        return rcopy(h.at[half, t], h.at[half, t], gxz_s.at[yy], gx_r.at[half, yy], to)

    def c_copy(x_lo, yy, cc, half):
        t = x_lo * 16 + yy * 2 + cc
        i = x_lo * 8 + yy
        return rcopy(h.at[half, t], h.at[half, t], gc_s.at[half, i], gc_r.at[half, i], partner)

    def rows_of(i, cc):
        return pl.ds(pl.multiple_of((i * 2 + cc) * SH, 16), SH)

    def w_copy(i):
        return rcopy(wt.at[rows_of(i, 1 - c)], wt_in.at[i], w_s.at[i], w_r.at[i], partner)

    term_copy = rcopy(term, term_in, m_s, m_r, partner)

    def to_x(half, yy, way):
        return rcopy(xtx.at[half, yy], xrx.at[half, yy], x_s.at[half, yy], x_r.at[half, yy], dev(x + way, y, z, c))

    def to_z(x_lo, yy):
        return rcopy(ztx.at[x_lo, yy], zrx.at[x_lo, yy], z_s.at[x_lo, yy], z_r.at[x_lo, yy], dev(x, y, z + along(yy), c))

    def to_x_t(half, yy, way):
        return rcopy(xtx_t.at[half, yy], xrx_t.at[half, yy], xt_s.at[half, yy], xt_r.at[half, yy], dev(x + way, y, z, c))

    def to_z_t(x_lo, yy):
        return rcopy(ztx_t.at[x_lo, yy], zrx_t.at[x_lo, yy], zt_s.at[x_lo, yy], zt_r.at[x_lo, yy], dev(x, y, z + along(yy), c))

    def to_y(frm, to, a):
        rows = pl.ds(pl.multiple_of(64 * lax.rem(x_hi + a, 2), 16), PART)
        return rcopy(ytx.at[to, rows], yrx.at[x_hi, frm], y_s.at[a, to], y_r.at[x_hi, frm], dev(x + 2 * a, to, z, c))

    def from_y(frm, a):
        other_hi = lax.rem(x_hi + a, 2)
        return rcopy(ytx.at[0, pl.ds(0, PART)], yrx.at[other_hi, frm], y_s.at[a, frm], y_r.at[other_hi, frm], dev(x + 2 * a, frm, z, c))

    def at_y(d):
        return lax.rem(y + d, 8)

    def part_a(k):
        return lax.div(k, 2) * 4 + lax.rem(k, 2)

    def part_b(k):
        return part_a(k) + 2

    def halves(value):
        low, high = value[:, 0:128], value[:, 128:256]
        return jnp.where(first, low, high), jnp.where(first, high, low)

    def from_mine(i, ref):
        return jnp.dot(wt[rows_of(i, c), :], ref[...], preferred_element_type=F32)

    def from_theirs(i, ref):
        return jnp.dot(wt_in[i], ref[...], preferred_element_type=F32)

    for d in NEAR:
        y_copy(y, at_y(d)).start()
    for half in range(2):
        x_copy(q, y, half).start()
        c_copy(q, y, c, half).start()

    loads[4].wait()
    for j in range(D // 128):
        wt[j * 128 : (j + 1) * 128, :] = jnp.transpose(w[:, j * 128 : (j + 1) * 128], (1, 0))

    def start_w(i, _):
        w_copy(i).start()
        return 0

    lax.fori_loop(0, 16, start_w, 0)
    for load in loads[1:4]:
        load.wait()
    slot_target = slot_lanes(tgt, tgt_wide, pln, -1, jnp.int32)
    slot_grad = slot_lanes(grd, grd_wide, pln, 0.0, F32)
    s_id, t_id = lax.axis_index("section"), lax.axis_index("tensor")
    entry = lax.broadcasted_iota(jnp.int32, (V, 256), 0)
    hit = (s_id * 32 + t_id) * V + entry == slot_target
    hot[...] = hit.astype(F32).astype(BF16)
    hot_in[...] = ((s_id * 32 + t_id + 1 - 2 * c) * V + entry == slot_target).astype(F32).astype(BF16)

    def target_rows(i):
        w_copy(i).wait_recv()
        return from_mine(i, hot) + from_theirs(i, hot_in)

    def target_first(k, _):
        ya, yb = part_a(k), part_b(k)
        value = target_rows(other * 8 + ya).astype(BF16)
        for half in range(2):
            xtx_t[half, ya] = value[:, half * 128 : (half + 1) * 128]
            to_x_t(half, ya, 1 - 2 * half).start()
        for x_lo in (other, q):
            i = x_lo * 8 + yb
            keep, pass_on = halves(target_rows(i))
            ztx_t[x_lo, yb] = pass_on.astype(BF16)
            to_z_t(x_lo, yb).start()
            own_t[i, :, 0:128] = keep.astype(BF16)
        return 0

    def target_keep(k, _):
        i = q * 8 + part_a(k)
        own_t[i] = target_rows(i).astype(BF16)
        return 0

    for d in NEAR:
        yy = at_y(d)
        y_copy(yy, y).wait_recv()
        x_copy(q, yy, p).start()
        xz_copy(q, yy, p).start()
        z_copy(yy, p).start()
        c_copy(q, yy, c, p).start()
    for n, d in enumerate(NEAR):
        yy = at_y(d)
        z_copy(yy, 1 - p).wait_recv()
        c_copy(q, yy, c, 1 - p).start()
        x_copy(other, yy, p).wait_recv()
        c_copy(other, yy, c, p).start()
        if n < 4:
            target_first(n, 0)
        elif n < 6:
            lax.fori_loop(2 * n - 8, 2 * n - 6, target_keep, 0)
    x_copy(other, y, p).wait_recv()
    c_copy(other, y, c, p).start()
    for d in (0,) + NEAR:
        yy = at_y(d)
        x_copy(other, yy, 1 - p).wait_recv()
        c_copy(other, yy, c, 1 - p).start()

    def target_second(k, _):
        ya, yb = part_a(k), part_b(k)
        to_z_t(other, yb).wait_recv()
        xtx_t[0, yb] = own_t[other * 8 + yb, :, 0:128] + zrx_t[other, yb]
        to_x_t(0, yb, along(yb)).start()
        i = q * 8 + ya
        for half in range(2):
            to_x_t(half, ya, 1 - 2 * half).wait_recv()
        both = own_t[i] + jnp.concatenate([xrx_t[0, ya], xrx_t[1, ya]], axis=1)
        keep, pass_on = halves(both.astype(F32))
        ztx_t[0, ya] = pass_on.astype(BF16)
        to_z_t(0, ya).start()
        own_t[i, :, 0:128] = keep.astype(BF16)
        return 0


    def columns(b):
        return jnp.concatenate(
            [h[half, pl.ds(b * 8, 8)].reshape(8 * SH, 128) for half in range(2)], axis=1
        )

    def blocks(i, raw):
        b = lax.rem(q * 2 + i, 4)
        x_lo = lax.div(b, 2)
        for k in range(4):
            for half in range(2):
                c_copy(x_lo, lax.rem(b, 2) * 4 + k, 1 - c, half).wait_recv()
        part = w[:, pl.ds(pl.multiple_of(b * 8 * SH, 128), 8 * SH)]
        return raw + jnp.dot(part, columns(b), preferred_element_type=F32)

    raw = lax.fori_loop(0, 4, blocks, jnp.zeros((V, 256), F32))
    capped = CAP * jnp.tanh(raw / CAP)
    exponent = jnp.exp(capped)
    curve = 1.0 - jnp.square(capped / CAP)
    sums = jnp.concatenate(
        [
            jnp.sum(exponent, axis=0, keepdims=True),
            jnp.sum(jnp.where(hit, capped, 0.0), axis=0, keepdims=True),
        ],
        axis=0,
    )

    def member_of(stage, j):
        if stage == 0:
            return dev(lax.div(j, 2), y, z, lax.rem(j, 2))
        return dev(x, j, z, c) if stage == 1 else dev(x, y, j, c)

    index_of = (x * 2 + c, y, z)

    def tot_copy(stage, frm, d):
        to = member_of(stage, lax.rem(index_of[stage] + d, 8))
        return rcopy(tot_tx.at[stage], tot_rx.at[stage, frm], t_s.at[stage, d], t_r.at[stage, frm], to)

    def begin(stage, values):
        tot_tx[stage] = values
        tot_rx[stage, index_of[stage]] = values
        for d in FAR:
            tot_copy(stage, index_of[stage], d).start()

    def end(stage):
        for d in FAR:
            tot_copy(stage, lax.rem(index_of[stage] + d, 8), d).wait()
        total = tot_rx[stage, 0]
        for j in range(1, 8):
            total = total + tot_rx[stage, j]
        return total

    begin(0, sums)
    term[...] = jnp.where(hit, 0.0, exponent * curve).astype(BF16)
    term_copy.start()

    def mine_first(k, _):
        for i in (other * 8 + part_a(k), other * 8 + part_b(k), q * 8 + part_b(k)):
            own[i] = from_mine(i, term)
        return 0

    lax.fori_loop(0, 4, mine_first, 0)
    lax.fori_loop(0, 4, target_second, 0)
    term_copy.wait_recv()

    def send_first(k, _):
        ya, yb = part_a(k), part_b(k)
        value = own[other * 8 + ya] + from_theirs(other * 8 + ya, term_in)
        for half in range(2):
            xtx[half, ya] = value[:, half * 128 : (half + 1) * 128].astype(BF16)
            to_x(half, ya, 1 - 2 * half).start()
        for x_lo in (other, q):
            i = x_lo * 8 + yb
            keep, pass_on = halves(own[i] + from_theirs(i, term_in))
            ztx[x_lo, yb] = pass_on.astype(BF16)
            to_z(x_lo, yb).start()
            own[i, :, 0:128] = keep
        return 0

    lax.fori_loop(0, 2, send_first, 0)
    begin(1, end(0))
    lax.fori_loop(2, 4, send_first, 0)

    def keep_first(k, _):
        i = q * 8 + part_a(k)
        own[i] = from_mine(i, term) + from_theirs(i, term_in)
        return 0

    lax.fori_loop(0, 4, keep_first, 0)

    def send_second(k, _):
        ya, yb = part_a(k), part_b(k)
        to_z(other, yb).wait_recv()
        xtx[0, yb] = (own[other * 8 + yb, :, 0:128] + zrx[other, yb].astype(F32)).astype(BF16)
        to_x(0, yb, along(yb)).start()
        i = q * 8 + ya
        both = own[i]
        for half in range(2):
            to_x(half, ya, 1 - 2 * half).wait_recv()
        both = both + jnp.concatenate([xrx[0, ya], xrx[1, ya]], axis=1).astype(F32)
        keep, pass_on = halves(both)
        ztx[0, ya] = pass_on.astype(BF16)
        to_z(0, ya).start()
        own[i, :, 0:128] = keep
        return 0

    begin(2, end(1))
    lax.fori_loop(0, 4, send_second, 0)

    def ready_a(k, _):
        i, yy = q * 8 + part_a(k), part_a(k)
        to_z(0, yy).wait_recv()
        own[i, :, 0:128] = own[i, :, 0:128] + zrx[0, yy].astype(F32)
        return 0

    def ready_b(k, _):
        i, yy = q * 8 + part_b(k), part_b(k)
        to_z(q, yy).wait_recv()
        to_x(0, yy, along(yy)).wait_recv()
        own[i, :, 0:128] = own[i, :, 0:128] + zrx[q, yy].astype(F32) + xrx[0, yy].astype(F32)
        return 0

    def ready_t(k, _):
        i, yy = q * 8 + part_a(k), part_a(k)
        to_z_t(0, yy).wait_recv()
        own_t[i, :, 0:128] = own_t[i, :, 0:128] + zrx_t[0, yy]
        i, yy = q * 8 + part_b(k), part_b(k)
        to_z_t(q, yy).wait_recv()
        to_x_t(0, yy, along(yy)).wait_recv()
        own_t[i, :, 0:128] = own_t[i, :, 0:128] + zrx_t[q, yy] + xrx_t[0, yy]
        return 0

    lax.fori_loop(0, 4, ready_t, 0)
    lax.fori_loop(0, 4, ready_a, 0)
    lax.fori_loop(0, 4, ready_b, 0)
    sums = end(2)
    total, target_logit = sums[0:1], sums[1:2]
    target_curve = 1.0 - jnp.square(target_logit / CAP)
    coef_t = slot_grad * (1.0 - jnp.exp(target_logit) / total) * target_curve
    coef_s = slot_grad / total
    half_t = jnp.where(first, coef_t[:, 0:128], coef_t[:, 128:256])
    half_s = jnp.where(first, coef_s[:, 0:128], coef_s[:, 128:256])

    def merged(yy):
        i = q * 8 + yy
        return half_t * own_t[i, :, 0:128].astype(F32) - half_s * own[i, :, 0:128]

    def send_y(k, _):
        yy = lax.rem(y + k, 8)
        ytx[yy] = merged(yy).astype(BF16)
        to_y(y, yy, 0).start()
        to_y(y, yy, 1).start()
        return 0

    lax.fori_loop(1, 8, send_y, 0)
    mine = merged(y)
    ytx[y] = mine.astype(BF16)
    to_y(y, y, 1).start()
    own[q * 8 + y, :, 0:128] = mine
    acc = own[q * 8 + y, pl.ds(pl.multiple_of(64 * x_hi, 16), PART), 0:128]

    soft = (-(slot_grad * (exponent / total)) * curve).astype(BF16)

    def grad_block(b, _):
        wg[:, pl.ds(pl.multiple_of(b * 8 * SH, 128), 8 * SH)] = lax.dot_general(
            soft, columns(b), (((1,), (1,)), ((), ())), preferred_element_type=F32
        ).astype(BF16)
        return 0

    lax.fori_loop(0, 4, grad_block, 0)
    wg_copy = pltpu.make_async_copy(wg, weight_grad_ref, o_sem)
    wg_copy.start()
    logprob = target_logit - jnp.log(total)
    scale = slot_grad * target_curve
    for m in range(MICRO):
        for value, out in ((logprob, logprob_ref), (scale, scale_ref)):
            row = jnp.zeros((1, ROWS), F32)
            for k in range(MICRO):
                row = jnp.where(pln[k] == m, value[:, k * SLOT : k * SLOT + ROWS], row)
            out[m : m + 1, :] = row

    for d in NEAR:
        yy = at_y(d)
        for a in range(2):
            from_y(yy, a).wait_recv()
            acc = acc + yrx[lax.rem(x_hi + a, 2), yy].astype(F32)
    from_y(y, 1).wait_recv()
    acc = acc + yrx[1 - x_hi, y].astype(F32)

    atx[...] = acc.astype(BF16)
    arx[x_hi, z] = atx[...]
    mates = [(a, d) for d in FAR + (0,) for a in range(2) if a or d]

    def to_mate(n, a, d):
        return rcopy(atx, arx.at[x_hi, z], a_s.at[n], a_r.at[n], dev(x + 2 * a, y, z + d, c))

    def from_mate(n, a, d):
        there = arx.at[lax.rem(x_hi + a, 2), lax.rem(z - d + 8, 8)]
        return rcopy(atx, there, a_s.at[n], a_r.at[n], dev(x + 2 * a, y, z - d, c))

    for n, (a, d) in enumerate(mates):
        to_mate(n, a, d).start()

    for d in FAR:
        y_copy(y, at_y(d)).wait_send()
    for d in NEAR:
        z_copy(at_y(d), p).wait_send()
        x_copy(q, at_y(d), p).wait_send()
        xz_copy(q, at_y(d), p).wait_send()
    for d in (0,) + NEAR:
        for half in range(2):
            for x_lo in range(2):
                c_copy(x_lo, at_y(d), c, half).wait_send()
    for half in range(2):
        x_copy(q, y, half).wait_send()
    term_copy.wait_send()

    def drain(yy, _):
        for x_lo in range(2):
            w_copy(x_lo * 8 + yy).wait_send()
        return 0

    def drain_ab(k, _):
        ya, yb = part_a(k), part_b(k)
        for half in range(2):
            to_x(half, ya, 1 - 2 * half).wait_send()
            to_z(half, yb).wait_send()
            to_x_t(half, ya, 1 - 2 * half).wait_send()
            to_z_t(half, yb).wait_send()
        to_z(0, ya).wait_send()
        to_x(0, yb, along(yb)).wait_send()
        to_z_t(0, ya).wait_send()
        to_x_t(0, yb, along(yb)).wait_send()
        return 0

    lax.fori_loop(0, 8, drain, 0)
    lax.fori_loop(0, 4, drain_ab, 0)
    for d in FAR:
        for a in range(2):
            to_y(y, at_y(d), a).wait_send()
    to_y(y, y, 1).wait_send()
    wg_copy.wait()
    for n, (a, d) in enumerate(mates):
        from_mate(n, a, d).wait_recv()
        to_mate(n, a, d).wait_send()
    for half in range(2):
        parts = []
        for hi in range(2):
            part = arx[hi, half].astype(F32)
            for k in range(1, 4):
                part = part + arx[hi, 2 * k + half].astype(F32)
            parts.append(part)
        wide = jnp.concatenate([parts[0], parts[1][2 * PART - SH :], jnp.zeros((256 - SH, 128), F32)], axis=0)
        flat = jnp.transpose(wide, (1, 0))
        for k in range(2):
            spread[:, half * 2 + k, :] = flat[k * SLOT : k * SLOT + ROWS, 0:SH]
    hidden_grad_ref[...] = spread[...].astype(BF16)


def hand_on_kernel(a0, a1, a2, a3, b0, b1, b2, b3, v0, v1, v2, v3, sem_in, sem_out):
    cuts = [(0, 64), (64, 64), (128, 64), (192, 80)]
    pieces = [(a0.at[pl.ds(i, n)], v0.at[pl.ds(i, n)], b0.at[pl.ds(i, n)]) for i, n in cuts]
    pieces += [(a1, v1, b1), (a2, v2, b2), (a3, v3, b3)]
    reads = [pltpu.make_async_copy(a, v, sem_in.at[i]) for i, (a, v, b) in enumerate(pieces)]
    writes = [pltpu.make_async_copy(v, b, sem_out.at[i]) for i, (a, v, b) in enumerate(pieces)]
    for read in reads:
        read.start()
    for read, write in zip(reads, writes):
        read.wait()
        write.start()
    for write in writes:
        write.wait()


def per_device(hidden, weight, targets, plan, row_grad):
    vmem = pl.BlockSpec(memory_space=pltpu.VMEM)
    hbm = pl.BlockSpec(memory_space=pl.ANY)
    dma = pltpu.SemaphoreType.DMA
    piece = (SH, 128)
    outs = (
        jax.ShapeDtypeStruct((V, D), BF16),
        jax.ShapeDtypeStruct((ROWS, MICRO, SH), BF16),
        jax.ShapeDtypeStruct((MICRO, ROWS), F32),
        jax.ShapeDtypeStruct((MICRO, ROWS), F32),
    )
    def buf(*shape, dtype=BF16):
        return pltpu.VMEM(shape, dtype)

    results = pl.pallas_call(
        comm_kernel,
        out_shape=outs,
        in_specs=[hbm] * 5,
        out_specs=(hbm, vmem, vmem, vmem),
        scratch_shapes=[
            buf(ROWS, MICRO, SH), buf(MICRO, ROWS, dtype=jnp.int32), buf(MICRO, ROWS, dtype=F32),
            pltpu.SMEM((MICRO,), jnp.int32),
            buf(MICRO, 128, dtype=jnp.int32), buf(MICRO, 128, dtype=F32),
            buf(ROWS, MICRO, SH, dtype=F32), buf(256, 256, dtype=F32),
            buf(2, 32, *piece), buf(V, D), buf(D, V), buf(16, SH, V), buf(V, D),
            buf(V, 256), buf(V, 256), buf(V, 256), buf(V, 256),
            buf(16, SH, 256, dtype=F32), buf(2, 8, *piece), buf(2, 8, *piece), buf(2, 8, *piece), buf(2, 8, *piece),
            buf(16, SH, 256), buf(2, 8, *piece), buf(2, 8, *piece), buf(2, 8, *piece), buf(2, 8, *piece),
            buf(8, *piece), buf(2, 8, PART, 128), buf(PART, 128), buf(2, 8, PART, 128),
            buf(3, 2, 256, dtype=F32), buf(3, 8, 2, 256, dtype=F32),
            dma((5,)), dma,
            dma((8,)), dma((8,)), dma((8,)), dma((8,)), dma((2, 8)), dma((2, 8)), dma((8,)), dma((2, 16)), dma((2, 16)),
            dma((3, 8)), dma((3, 8)), dma((16,)), dma((16,)), dma, dma,
            dma((2, 8)), dma((2, 8)), dma((2, 8)), dma((2, 8)), dma((2, 8)), dma((2, 8)), dma((2, 8)), dma((2, 8)),
            dma((2, 8)), dma((2, 8)), dma((15,)), dma((15,)),
        ],
        compiler_params=pltpu.CompilerParams(collective_id=0, has_side_effects=True, vmem_limit_bytes=62 << 20),
        name="gather_logits_reduce",
    )(jnp.transpose(hidden, (1, 0, 2)), weight, targets, plan, row_grad)
    weight_grad, hidden_grad, logprob, scale = pl.pallas_call(
        hand_on_kernel,
        out_shape=outs,
        in_specs=[hbm] * 4,
        out_specs=(hbm,) * 4,
        scratch_shapes=[pltpu.VMEM(out.shape, out.dtype) for out in outs] + [dma((7,)), dma((7,))],
        compiler_params=pltpu.CompilerParams(vmem_limit_bytes=62 << 20),
        name="hand_on",
    )(*results)
    return logprob, jnp.transpose(hidden_grad, (1, 0, 2)), weight_grad, scale


def solution(mesh):
    placed = (P(None, None, "tensor"), P(("section", "tensor"), None), P(), P(), P())
    return jax.shard_map(
        per_device,
        mesh=mesh,
        in_specs=placed,
        out_specs=(P(), P(None, None, "tensor"), P(("section", "tensor"), None), P()),
        check_vma=False,
    )
```
